256 devices in a mesh: sec: 4 (over y), rep: 32 (over x, z_lo, core), blk: 2 (over z_hi).
Axes of the slice: x: 4, y: 4, z: 8 (z_hi: 2, z_lo: 4; z = z_hi * 4 + z_lo), core: 2. Of those that a mesh axis runs over, the one named last changes fastest.
Arguments:
- observations: bfloat16 [4096, 32, 256], P(('sec', 'rep')), may hold values from -6 to 6
- in_weight: bfloat16 [256, 4, 2048], P(None, None, 'blk'), may hold values from -0.375 to 0.375
- rec_blocks: bfloat16 [4, 16, 4, 128, 128], P(None, 'blk'), may hold values from -0.25 to 0.25
- block_rows: int32 [4, 16, 4], P(None, 'blk'), may hold values from 0 to 15, as said below
- episode_start: int32 [4096, 32], P(('sec', 'rep')), may hold values 0 or 1
- actions: int32 [4096, 32], P(('sec', 'rep')), may hold values from 0 to 15
- rewards: float32 [4096, 32], P(('sec', 'rep')), may hold values from -6 to 6
- mu_logp: float32 [4096, 32], P(('sec', 'rep')), may hold values from -4 to -1.5
- head_weight: bfloat16 [2048, 17], P('blk'), may hold values from -0.25 to 0.25
- learner_of: int32 [4096, 1], P(('sec', 'rep')), may hold values from 0 to 31; in each aligned block of 32 rows (0 to 31, 32 to 63, ...) at most 2 rows name the same one
Outputs:
- head_grad: float32 [2048, 17], P('blk')
- hidden_last: bfloat16 [4096, 2048], P(('sec', 'rep'), 'blk')
- cell_last: float32 [4096, 2048], P(('sec', 'rep'), 'blk')
The draws below stay inside these ranges and needn't reach their ends.
Inputs may be any that keep to these rules, and one draw needn't show every extreme that they name: `block_rows`: the 4 block rows of one gate's block column are distinct. `learner_of`: among the 32 agents of one device, at most 2 have the same learner, and some learner has exactly 2.
All inputs are finite; a program needn't handle non-finite values. No bound on the sum of `episode_start` on one device may be relied on, other than what follows from the above.
Results may differ from the reference program's by a relative error of at most 0.0045.
Values may be sent and summed in bfloat16 or wider, within the bound.
No kernel may reach another device: no remote copies, remote signals or barrier semaphores. Data moves between devices by JAX's collectives and lax.ppermute only.
A program may use at most 128 MiB of HBM per device.

```python
import math
import jax
import jax.numpy as jnp
import numpy as np
from jax import lax

H = 2048
OBS = 256
ACT = 16
BS = 128
STEPS = 32
A_DEV = 32
NBC = 16
KB = 4
AGENTS = 4096
CAP = 2
N_SEC = 4
N_REP = 32


def draw_block_rows(key, part):
    keys = jax.random.split(key, 4 * NBC)
    perms = jax.vmap(lambda k: jax.random.permutation(k, NBC))(keys)
    return perms[:, :KB].reshape(4, NBC, KB).astype(jnp.int32)


def set_ends(values, stream_key, smallest, largest):
    longest = values.shape.index(max(values.shape))
    spots = []
    for shift in (0, 1):
        where = [jax.random.randint(jax.random.fold_in(stream_key, axis), (), 0, length) for axis, length in enumerate(values.shape)]
        where[longest] = (where[longest] + shift) % values.shape[longest]
        spots.append(tuple(where))
    return values.at[spots[0]].set(smallest).at[spots[1]].set(largest)


def level_of(own_key, extent, cuts, low, largest):
    factor_of = 1.0
    for dim, shards_of in cuts:
        draws = jax.random.uniform(jax.random.fold_in(jax.random.fold_in(own_key, 6), dim), (shards_of,), jnp.float32, low / len(cuts), largest / len(cuts))
        factor_of = factor_of * jnp.repeat(jnp.exp(draws), extent[dim] // shards_of).reshape((-1,) + (1,) * (len(extent) - 1 - dim))
    return factor_of


def assign_block(rng, own, number, rows, amount, top, bound, skew):
    ranking = jax.random.permutation(rng, amount)
    heavy_load, usual = portions_of(amount, rows * top, bound, skew, True), portions_of(amount, rows * top, bound, skew, False)
    places = jnp.arange(amount)

    def named(tallies, offset_by):
        used = int((tallies > 0).sum())
        fixed = max(1, used // 4)
        moved = fixed + (places - fixed + offset_by * (used - fixed)) % max(1, amount - fixed)
        return jnp.zeros((amount,), jnp.int32).at[ranking[jnp.where(places < fixed, places, moved)]].set(jnp.asarray(tallies, jnp.int32))

    tallies = jnp.where(number % 4 == 0, named(heavy_load, number // 4), named(usual, number - number // 4 - 1))
    mixed = jax.random.permutation(jax.random.fold_in(own, 3), amount)
    source_of, taker = mixed[0:amount // 2 * 2:2], mixed[1:amount // 2 * 2:2]
    slack = jnp.minimum(tallies[source_of] - 1, bound - tallies[taker]) // 2
    slack = jnp.where((source_of == ranking[0]) | (taker == ranking[0]) | (tallies[taker] == 0), 0, jnp.maximum(slack, 0))
    moved = jax.random.randint(jax.random.fold_in(own, 4), (amount // 2,), 0, 1 << 20) % (slack + 1)
    tallies = tallies.at[source_of].add(-moved).at[taker].add(moved)
    members = jnp.searchsorted(jnp.cumsum(tallies), jnp.arange(rows * top), side="right").astype(jnp.int32)
    listing = members.reshape(top, rows).T
    listing = listing[jax.random.permutation(jax.random.fold_in(own, 1), rows)]
    offset_by = jax.random.randint(jax.random.fold_in(own, 2), (rows, 1), 0, top)
    return jnp.take_along_axis(listing, (jnp.arange(top)[None, :] + offset_by) % top, axis=1)


def portions_of(amount, total, reach, slope, full):
    weights = [(1 << 20) // math.isqrt(rank ** slope) + 1 for rank in range(1, amount + 1)]
    largest = reach if full else min(reach, max(-(-total // amount), total * weights[0] // sum(weights)))
    least = 1 if total - largest >= amount - 1 else 0
    given, rest = [largest] + [least] * (amount - 1), total - largest - least * (amount - 1)
    while rest > 0:
        candidates = [i for i in range(1, amount) if given[i] < largest] or [i for i in range(1, amount) if given[i] < reach]
        whole, budget = sum([weights[i] for i in candidates]), rest
        for i in candidates:
            extra = min(reach - given[i], max(1, budget * weights[i] // whole), rest)
            given[i] = given[i] + extra
            rest = rest - extra
    return np.array(given)


def centred(own_key, dims, deviation, bound, shards=(), held_as=jnp.bfloat16):
    values = jax.random.normal(own_key, dims, jnp.float32) * deviation
    if len(shards) > 0:
        values = level_of(own_key, dims, shards, -0.22, 0.18) * values
    return jnp.clip(values, min=-bound, max=bound).astype(held_as)


def setup_inputs(seed: int = 0) -> dict:
    splits = jax.random.split(jax.random.key(seed), 11)
    observations = centred(splits[0], (AGENTS, STEPS, OBS), 1.0, 6.0, ((0, 128),))
    in_weight = centred(splits[1], (OBS, 4, H), OBS ** -0.5, 0.375, ((2, 2),))
    rec_blocks = centred(splits[2], (4, NBC, KB, BS, BS), (KB * BS) ** -0.5, 0.25, ((1, 2),))
    block_rows = draw_block_rows(jax.random.fold_in(splits[10], 71), 0)
    episode_start = set_ends((jax.random.randint(splits[4], (AGENTS, STEPS), 0, 16) < 1).astype(jnp.int32), jax.random.fold_in(splits[4], 1), 0, 1)
    actions = set_ends(jax.random.randint(splits[5], (AGENTS, STEPS), 0, ACT), jax.random.fold_in(splits[5], 1), 0, ACT - 1).astype(jnp.int32)
    rewards = centred(splits[6], (AGENTS, STEPS), 1.0, 6.0, ((0, 128),), jnp.float32)
    mu_logp = jnp.clip(-4.0 + 2.5 * jax.random.uniform(splits[7], (AGENTS, STEPS), jnp.float32) ** level_of(splits[7], (AGENTS, STEPS), ((0, 128),), -0.2, 0.2), -4.0, -1.5)
    head_weight = centred(splits[8], (H, ACT + 1), (H // 4) ** -0.5, 0.25, ((0, 2),))
    learner_of_keys = jax.random.split(jax.random.fold_in(splits[9], 1), AGENTS // A_DEV)
    learner_of_turns = jax.random.permutation(jax.random.fold_in(splits[9], 3), AGENTS // A_DEV)
    learner_of = jax.vmap(lambda own, number: assign_block(jax.random.fold_in(splits[9], 2), own, number, A_DEV, N_REP, 1, CAP, 2))(learner_of_keys, learner_of_turns).reshape((AGENTS, 1))
    return dict(observations=observations, in_weight=in_weight, rec_blocks=rec_blocks, block_rows=block_rows, episode_start=episode_start, actions=actions, rewards=rewards, mu_logp=mu_logp, head_weight=head_weight, learner_of=learner_of)


GAMMA_RATE = 0.99


def backward_sum(td_delta, factor):
    def stepper(accum_next, inputs):
        delta_now, factor_now = inputs
        accum_now = delta_now + factor_now * accum_next
        return accum_now, accum_now
    start_val = jnp.zeros((td_delta.shape[0],), jnp.float32)
    _, accums = lax.scan(stepper, start_val, (td_delta.T, factor.T), reverse=True)
    return accums.T


def learner_terms(head_out, rewards, mu_logp, actions, starts, weight):
    num_actions = head_out.shape[-1] - 1
    logits = head_out[..., :num_actions]
    value_est = head_out[..., num_actions]
    top_val = jnp.max(logits, axis=-1, keepdims=True)
    shifted = jnp.exp(logits - top_val)
    total = jnp.sum(shifted, axis=-1, keepdims=True)
    policy_probs = shifted / total
    log_total = jnp.log(total)[..., 0] + top_val[..., 0]
    picked = (actions[..., None] == jnp.arange(num_actions).astype(actions.dtype)).astype(jnp.float32)
    logp = jnp.sum(picked * logits, axis=-1) - log_total
    clipped_rho = jnp.minimum(1.0, jnp.exp(logp - mu_logp))
    next_start = jnp.concatenate([starts[:, 1:], jnp.zeros_like(starts[:, :1])], axis=1)
    discount = GAMMA_RATE * (1.0 - next_start)
    value_next = jnp.concatenate([value_est[:, 1:], value_est[:, -1:]], axis=1)
    td_delta = clipped_rho * (rewards + discount * value_next - value_est)
    accum = backward_sum(td_delta, discount * clipped_rho)
    targets = value_est + accum
    target_next = jnp.concatenate([targets[:, 1:], value_est[:, -1:]], axis=1)
    advantage = clipped_rho * (rewards + discount * target_next - value_est)
    d_logits = -(weight[:, None] * advantage)[..., None] * (picked - policy_probs)
    d_value = weight[:, None] * (value_est - targets)
    return jnp.concatenate([d_logits, d_value[..., None]], axis=-1).astype(jnp.bfloat16)


def reference(observations, in_weight, rec_blocks, block_rows, episode_start, actions, rewards, mu_logp, head_weight, learner_of):
    num_agents = observations.shape[0]
    in_terms = jnp.einsum('asd,dgh->sagh', observations.astype(jnp.float32), in_weight.astype(jnp.float32))
    starts = episode_start.astype(jnp.float32)
    blocks_f = rec_blocks.astype(jnp.float32)

    def advance(state_pair, inputs):
        hidden, cell_state = state_pair
        in_step, start_step = inputs
        keep_mask = 1.0 - start_step[:, None]
        hidden_in = (hidden.astype(jnp.float32) * keep_mask)
        cell_in = cell_state * keep_mask
        picked_rows = hidden_in.reshape(num_agents, NBC, BS)[:, block_rows]
        rec_terms = jnp.einsum('agckb,gckbe->agce', picked_rows, blocks_f).reshape(num_agents, 4, H)
        gate_terms = in_step + rec_terms
        gate_in = jax.nn.sigmoid(gate_terms[:, 0])
        gate_forget = jax.nn.sigmoid(gate_terms[:, 1])
        update = jnp.tanh(gate_terms[:, 2])
        gate_out = jax.nn.sigmoid(gate_terms[:, 3])
        new_cell = gate_forget * cell_in + gate_in * update
        new_hidden = (gate_out * jnp.tanh(new_cell)).astype(jnp.bfloat16)
        return (new_hidden, new_cell), new_hidden

    start_pair = (jnp.zeros((num_agents, H), jnp.bfloat16), jnp.zeros((num_agents, H), jnp.float32))
    (hidden_last, cell_last), trajectory = lax.scan(advance, start_pair, (in_terms, starts.T))
    traj_f = trajectory.astype(jnp.float32)
    head_out = jnp.einsum('sah,hk->ask', traj_f, head_weight.astype(jnp.float32))
    onehot = (learner_of[:, 0][:, None] == jnp.arange(N_REP).astype(learner_of.dtype)).astype(jnp.float32)
    grouped = onehot.reshape(N_SEC, -1, N_REP)
    counts = jnp.sum(grouped, axis=1)
    agent_count = jnp.sum(grouped * counts[:, None, :], axis=-1).reshape(num_agents)
    weight = 1.0 / (jnp.maximum(agent_count, 1.0) * STEPS)
    head_cot = learner_terms(head_out, rewards, mu_logp, actions.astype(jnp.float32), starts, weight)
    head_grad = jnp.einsum('sah,ask->hk', traj_f, head_cot.astype(jnp.float32))
    return head_grad, hidden_last, cell_last
```

```python
import jax
import jax.numpy as jnp
from jax import lax
from jax.experimental import pallas as pl
from jax.experimental.pallas import tpu as pltpu
from jax.sharding import Mesh, PartitionSpec as P

GAMMA_RATE = 0.99
BLOCK = 128
HEADS = 24
TORUS = ("y", "x", "z", "core")


def sigmoid(x):
    return 0.5 * jnp.tanh(0.5 * x) + 0.5


def rollout_kernel(
    rows_ref,
    obs_ref,
    keep_ref,
    side_ref,
    in_own_ref,
    rec_own_ref,
    head_own_ref,
    other_ref,
    grad_ref,
    hidden_ref,
    cell_ref,
    in_terms,
    state,
    cell,
    traj,
):
    steps, agents, _ = keep_ref.shape
    cols = state.shape[1]
    half = cols // 2
    lanes = steps * agents
    obs_width = obs_ref.shape[1]
    rec_rows = 4 * BLOCK
    head_at = obs_width + rec_rows

    def in_own(i, _):
        for g in range(4):
            w = in_own_ref[:, g, pl.ds(pl.multiple_of(i * 256, 256), 256)]
            out = jnp.dot(obs_ref[...], w, preferred_element_type=jnp.float32)
            for j in range(2):
                in_terms[g, 2 * i + j] = out[:, j * BLOCK : (j + 1) * BLOCK]
        return 0

    def in_other(i, _):
        for g in range(4):
            w = jnp.concatenate(
                [other_ref[g * half + 2 * i + j, :obs_width, :] for j in range(2)], axis=1
            )
            out = jnp.dot(obs_ref[...], w, preferred_element_type=jnp.float32)
            for j in range(2):
                in_terms[g, half + 2 * i + j] = out[:, j * BLOCK : (j + 1) * BLOCK]
        return 0

    lax.fori_loop(0, half // 2, in_own, 0)
    lax.fori_loop(0, half // 2, in_other, 0)

    state[0] = jnp.zeros_like(state[0])
    cell[...] = jnp.zeros_like(cell)

    def step(t, _):
        now = lax.rem(t, 2)
        base = pl.multiple_of(t * agents, agents)
        keep = keep_ref[jnp.minimum(t + 1, steps - 1)]
        for c in range(cols):
            pre = []
            for g in range(4):
                parts = [state[now, rows_ref[(g * cols + c) * 4 + k]] for k in range(4)]
                lhs = jnp.concatenate(parts, axis=1)
                if c < half:
                    rhs = rec_own_ref[g, c].reshape(rec_rows, BLOCK)
                else:
                    rhs = other_ref[g * half + c - half, obs_width:head_at, :]
                pre.append(
                    in_terms[g, c, pl.ds(base, agents), :]
                    + jnp.dot(lhs, rhs, preferred_element_type=jnp.float32)
                )
            new_cell = sigmoid(pre[1]) * cell[c] + sigmoid(pre[0]) * jnp.tanh(pre[2])
            new_hidden = (sigmoid(pre[3]) * jnp.tanh(new_cell)).astype(jnp.bfloat16)
            traj[c, pl.ds(base, agents), :] = new_hidden
            state[1 - now, c] = (new_hidden * keep).astype(jnp.bfloat16)
            cell_ref[:, c * BLOCK : (c + 1) * BLOCK] = new_cell
            cell[c] = new_cell * keep
        return 0

    lax.fori_loop(0, steps, step, 0)
    for c in range(cols):
        hidden_ref[:, c * BLOCK : (c + 1) * BLOCK] = traj[c, lanes - agents :, :]

    out = jnp.zeros((HEADS, lanes), jnp.float32)
    per = 4
    for c in range(cols):
        if c < half:
            head = head_own_ref[c * BLOCK : (c + 1) * BLOCK, :]
        else:
            first = (c - half) * per
            head = jnp.concatenate(
                [other_ref[first + j, head_at : head_at + BLOCK // per, :] for j in range(per)],
                axis=0,
            )
        out = out + lax.dot_general(
            jnp.transpose(head)[:HEADS],
            traj[c],
            (((1,), (1,)), ((), ())),
            preferred_element_type=jnp.float32,
        )
    logits = out[:16]
    value = out[16:17]
    side = side_ref[...]
    rewards, mu_logp, actions, next_start, weight = [side[i : i + 1] for i in range(5)]
    top = jnp.max(logits, axis=0, keepdims=True)
    shifted = jnp.exp(logits - top)
    total = jnp.sum(shifted, axis=0, keepdims=True)
    probs = shifted / total
    log_total = jnp.log(total) + top
    which = lax.broadcasted_iota(jnp.int32, logits.shape, 0).astype(jnp.float32)
    picked = (which == actions).astype(jnp.float32)
    logp = jnp.sum(picked * logits, axis=0, keepdims=True) - log_total
    rho = jnp.minimum(1.0, jnp.exp(logp - mu_logp))
    discount = GAMMA_RATE * (1.0 - next_start)
    lane = lax.broadcasted_iota(jnp.int32, value.shape, 1)
    last = lane >= lanes - agents

    def ahead(x, by):
        return pltpu.roll(x, lanes - by, 1)

    value_next = jnp.where(last, value, ahead(value, agents))
    acc = rho * (rewards + discount * value_next - value)
    factor = discount * rho
    by = agents
    while by < lanes:
        out_of = lane >= lanes - by
        acc = acc + factor * jnp.where(out_of, 0.0, ahead(acc, by))
        factor = factor * jnp.where(out_of, 0.0, ahead(factor, by))
        by *= 2
    targets = value + acc
    target_next = jnp.where(last, value, ahead(targets, agents))
    advantage = rho * (rewards + discount * target_next - value)
    d_logits = -(weight * advantage) * (picked - probs)
    d_value = weight * (value - targets)
    row = lax.broadcasted_iota(jnp.int32, (8, lanes), 0)
    d_tail = jnp.where(row == 0, d_value, 0.0)
    cot = jnp.concatenate([d_logits, d_tail], axis=0).astype(jnp.bfloat16)
    for c in range(cols):
        grad_ref[c // half, :, (c % half) * BLOCK : (c % half + 1) * BLOCK] = jnp.dot(
            cot, traj[c], preferred_element_type=jnp.float32
        )


def rollout(rows, obs, keep, side, in_own, rec_own, head_own, other):
    steps, agents, _ = keep.shape
    cols = 2 * rec_own.shape[1]
    width = cols * BLOCK
    vmem = pl.BlockSpec(memory_space=pltpu.VMEM)
    return pl.pallas_call(
        rollout_kernel,
        in_specs=[pl.BlockSpec(memory_space=pltpu.SMEM)] + [vmem] * 7,
        out_specs=[vmem] * 3,
        out_shape=[
            jax.ShapeDtypeStruct((2, HEADS, width // 2), jnp.float32),
            jax.ShapeDtypeStruct((agents, width), jnp.bfloat16),
            jax.ShapeDtypeStruct((agents, width), jnp.float32),
        ],
        scratch_shapes=[
            pltpu.VMEM((4, cols, steps * agents, BLOCK), jnp.float32),
            pltpu.VMEM((2, cols, agents, BLOCK), jnp.bfloat16),
            pltpu.VMEM((cols, agents, BLOCK), jnp.float32),
            pltpu.VMEM((cols, steps * agents, BLOCK), jnp.bfloat16),
        ],
        compiler_params=pltpu.CompilerParams(vmem_limit_bytes=60 * 1024 * 1024),
    )(rows, obs, keep, side, in_own, rec_own, head_own, other)


def swap(v):
    return lax.ppermute(v, "blk", [(0, 1), (1, 0)])


def butterfly(v, axes):
    for axis in axes:
        size = lax.axis_size(axis)
        k = 1
        while k < size:
            v = v + lax.ppermute(v, axis, [(i, i ^ k) for i in range(size)])
            k *= 2
    return v


def shards(
    observations,
    in_weight,
    rec_blocks,
    block_rows,
    episode_start,
    actions,
    rewards,
    mu_logp,
    head_weight,
    learner_of,
):
    blk = lax.axis_index("blk")
    num_agents, num_steps, obs_width = observations.shape
    mine = num_agents // 2
    cols = rec_blocks.shape[1]
    num_rep = 4 * cols
    rep = lax.axis_index(("x", "z", "core"))
    per = head_weight.shape[0] // num_rep

    head_own = jnp.pad(head_weight, ((0, 0), (0, BLOCK - head_weight.shape[1])))
    gate, col = rep // cols, rep % cols
    in_part = lax.dynamic_slice(in_weight, (0, gate, col * BLOCK), (obs_width, 1, BLOCK))
    rec_part = lax.dynamic_slice(
        rec_blocks, (gate, col, 0, 0, 0), (1, 1) + rec_blocks.shape[2:]
    )
    head_part = lax.dynamic_slice_in_dim(head_own, rep * per, per, 0)
    rows_part = jnp.broadcast_to(block_rows.reshape(1, -1), (16, BLOCK)).astype(jnp.bfloat16)
    packed = jnp.concatenate(
        [in_part.reshape(-1, BLOCK), rec_part.reshape(-1, BLOCK), head_part, rows_part], axis=0
    )
    other = lax.all_gather(swap(packed), ("x", "z", "core"))

    rows_other = other[0, -1, :].astype(jnp.int32).reshape(block_rows.shape)
    rows = jnp.concatenate([block_rows, rows_other], axis=1)
    rows = ((rows + cols * blk) % (2 * cols)).reshape(-1)

    onehot = (
        learner_of[:, 0][:, None] == jnp.arange(num_rep, dtype=jnp.int32)
    ).astype(jnp.float32)
    counts = butterfly(jnp.sum(onehot, axis=0), ("x", "z", "core"))
    agent_count = jnp.sum(onehot * counts[None, :], axis=1)
    weight = 1.0 / (jnp.maximum(agent_count, 1.0) * num_steps)

    starts = episode_start.astype(jnp.float32)
    next_start = jnp.concatenate([starts[:, 1:], jnp.zeros_like(starts[:, :1])], axis=1)
    side = jnp.stack(
        [
            rewards,
            mu_logp,
            actions.astype(jnp.float32),
            next_start,
            jnp.broadcast_to(weight[:, None], rewards.shape),
        ]
        + [jnp.zeros_like(rewards)] * 3
    )
    side = lax.dynamic_slice_in_dim(side, blk * mine, mine, 1)
    side = jnp.swapaxes(side, 1, 2).reshape(8, num_steps * mine)
    keep = 1.0 - lax.dynamic_slice_in_dim(starts, blk * mine, mine, 0).T[:, :, None]
    obs = lax.dynamic_slice_in_dim(observations, blk * mine, mine, 0)
    obs = jnp.swapaxes(obs, 0, 1).reshape(num_steps * mine, obs_width)

    grad, hidden, cell = rollout(
        rows, obs, keep, side, in_weight, rec_blocks, head_own, other
    )
    width = cols * BLOCK
    grad = butterfly(grad[0] + swap(grad[1]), TORUS)
    head_grad = grad[: head_weight.shape[1]].T

    def place(full):
        here, there = full[:, :width], swap(full[:, width:])
        first = jnp.where(blk == 0, here, there)
        second = jnp.where(blk == 0, there, here)
        return jnp.concatenate([first, second], axis=0)

    return (head_grad, place(hidden), place(cell))


def solution(mesh):
    fine = Mesh(mesh.devices.reshape(4, 4, 4, 2, 2), ("y", "x", "z", "core", "blk"))
    rows = TORUS
    return jax.shard_map(
        shards,
        mesh=fine,
        in_specs=(
            P(rows, None, None),
            P(None, None, "blk"),
            P(None, "blk", None, None, None),
            P(None, "blk", None),
            P(rows, None),
            P(rows, None),
            P(rows, None),
            P(rows, None),
            P("blk", None),
            P(rows, None),
        ),
        out_specs=(P("blk", None), P(rows, "blk"), P(rows, "blk")),
        check_vma=False,
    )
```

```python
import jax
import jax.numpy as jnp
from jax import lax
from jax.experimental import pallas as pl
from jax.experimental.pallas import tpu as pltpu
from jax.sharding import Mesh, PartitionSpec as P

GAMMA_RATE = 0.99
BLOCK = 128
HEADS = 24
HEAD_ROWS = 32
VMEM_LIMIT = 40 * 1024 * 1024
TORUS = ("y", "x", "z", "core")


def sigmoid(x):
    return 0.5 * jnp.tanh(0.5 * x) + 0.5


def input_kernel(obs_ref, weight_ref, out_ref):
    wide = 2 * BLOCK

    def body(i, _):
        for g in range(4):
            w = weight_ref[:, g, pl.ds(pl.multiple_of(i * wide, wide), wide)]
            out = jnp.dot(obs_ref[...], w, preferred_element_type=jnp.float32)
            for j in range(2):
                out_ref[g, 2 * i + j] = out[:, j * BLOCK : (j + 1) * BLOCK]
        return 0

    lax.fori_loop(0, weight_ref.shape[2] // wide, body, 0)


def input_terms(obs, weight):
    vmem = pl.BlockSpec(memory_space=pltpu.VMEM)
    return pl.pallas_call(
        input_kernel,
        in_specs=[vmem] * 2,
        out_specs=vmem,
        out_shape=jax.ShapeDtypeStruct(
            (4, weight.shape[2] // BLOCK, obs.shape[0], BLOCK), jnp.float32
        ),
        compiler_params=pltpu.CompilerParams(vmem_limit_bytes=VMEM_LIMIT),
    )(obs, weight)


def rollout_kernel(
    rows_ref,
    obs_ref,
    keep_ref,
    side_ref,
    terms_own_ref,
    rec_own_ref,
    head_own_ref,
    head_other_ref,
    other_ref,
    grad_own_ref,
    grad_other_ref,
    hidden_own_ref,
    hidden_other_ref,
    cell_own_ref,
    cell_other_ref,
    terms_other,
    state_a,
    state_b,
    cell,
    traj,
):
    steps, agents, _ = keep_ref.shape
    cols = traj.shape[0]
    half = cols // 2
    lanes = steps * agents
    obs_width = obs_ref.shape[1]
    rec_rows = 4 * BLOCK

    def in_other(i, _):
        for g in range(4):
            w = jnp.concatenate(
                [other_ref[g * half + 2 * i + j, :obs_width, :] for j in range(2)], axis=1
            )
            out = jnp.dot(obs_ref[...], w, preferred_element_type=jnp.float32)
            for j in range(2):
                terms_other[g, 2 * i + j] = out[:, j * BLOCK : (j + 1) * BLOCK]
        return 0

    lax.fori_loop(0, half // 2, in_other, 0)

    state_a[...] = jnp.zeros_like(state_a)
    cell[...] = jnp.zeros_like(cell)

    def step(t, state, state_next):
        base = pl.multiple_of(t * agents, agents)
        keep = keep_ref[jnp.minimum(t + 1, steps - 1)]
        for c in range(cols):
            own, cc = c < half, c % half
            terms_ref = terms_own_ref if own else terms_other
            cell_ref = cell_own_ref if own else cell_other_ref
            pre = []
            for g in range(4):
                parts = [state[rows_ref[(g * cols + c) * 4 + k]] for k in range(4)]
                lhs = jnp.concatenate(parts, axis=1)
                if own:
                    rhs = rec_own_ref[g, cc].reshape(rec_rows, BLOCK)
                else:
                    rhs = other_ref[g * half + cc, obs_width:, :]
                pre.append(
                    terms_ref[g, cc, pl.ds(base, agents), :]
                    + jnp.dot(lhs, rhs, preferred_element_type=jnp.float32)
                )
            new_cell = sigmoid(pre[1]) * cell[c] + sigmoid(pre[0]) * jnp.tanh(pre[2])
            new_hidden = (sigmoid(pre[3]) * jnp.tanh(new_cell)).astype(jnp.bfloat16)
            traj[c, pl.ds(base, agents), :] = new_hidden
            state_next[c] = (new_hidden * keep).astype(jnp.bfloat16)
            cell_ref[:, cc * BLOCK : (cc + 1) * BLOCK] = new_cell
            cell[c] = new_cell * keep

    def two_steps(i, _):
        step(2 * i, state_a, state_b)
        step(2 * i + 1, state_b, state_a)
        return 0

    lax.fori_loop(0, steps // 2, two_steps, 0)
    for c in range(cols):
        cc = c % half
        hidden_ref = hidden_own_ref if c < half else hidden_other_ref
        hidden_ref[:, cc * BLOCK : (cc + 1) * BLOCK] = traj[c, lanes - agents :, :]

    out = jnp.zeros((HEAD_ROWS, lanes), jnp.float32)
    for c in range(cols):
        head_ref, cc = (head_own_ref if c < half else head_other_ref), c % half
        out = out + lax.dot_general(
            head_ref[:, cc * BLOCK : (cc + 1) * BLOCK],
            traj[c],
            (((1,), (1,)), ((), ())),
            preferred_element_type=jnp.float32,
        )
    logits = out[:16]
    value = out[16:17]
    side = side_ref[...]
    rewards, mu_logp, actions, next_start, weight = [side[i : i + 1] for i in range(5)]
    top = jnp.max(logits, axis=0, keepdims=True)
    shifted = jnp.exp(logits - top)
    total = jnp.sum(shifted, axis=0, keepdims=True)
    probs = shifted / total
    log_total = jnp.log(total) + top
    which = lax.broadcasted_iota(jnp.int32, logits.shape, 0).astype(jnp.float32)
    picked = (which == actions).astype(jnp.float32)
    logp = jnp.sum(picked * logits, axis=0, keepdims=True) - log_total
    rho = jnp.minimum(1.0, jnp.exp(logp - mu_logp))
    discount = GAMMA_RATE * (1.0 - next_start)
    lane = lax.broadcasted_iota(jnp.int32, value.shape, 1)
    last = lane >= lanes - agents

    def ahead(x, by):
        return pltpu.roll(x, lanes - by, 1)

    value_next = jnp.where(last, value, ahead(value, agents))
    acc = rho * (rewards + discount * value_next - value)
    factor = discount * rho
    by = agents
    while by < lanes:
        out_of = lane >= lanes - by
        acc = acc + factor * jnp.where(out_of, 0.0, ahead(acc, by))
        factor = factor * jnp.where(out_of, 0.0, ahead(factor, by))
        by *= 2
    targets = value + acc
    target_next = jnp.where(last, value, ahead(targets, agents))
    advantage = rho * (rewards + discount * target_next - value)
    d_logits = -(weight * advantage) * (picked - probs)
    d_value = weight * (value - targets)
    row = lax.broadcasted_iota(jnp.int32, (8, lanes), 0)
    d_tail = jnp.where(row == 0, d_value, 0.0)
    cot = jnp.concatenate([d_logits, d_tail], axis=0).astype(jnp.bfloat16)
    for c in range(cols):
        grad_ref, cc = (grad_own_ref if c < half else grad_other_ref), c % half
        grad_ref[:, cc * BLOCK : (cc + 1) * BLOCK] = jnp.dot(
            cot, traj[c], preferred_element_type=jnp.float32
        )


def rollout(rows, obs, keep, side, terms_own, rec_own, head_own, head_other, other):
    steps, agents, _ = keep.shape
    half = rec_own.shape[1]
    cols, width, lanes = 2 * half, half * BLOCK, steps * agents
    vmem = pl.BlockSpec(memory_space=pltpu.VMEM)
    return pl.pallas_call(
        rollout_kernel,
        in_specs=[pl.BlockSpec(memory_space=pltpu.SMEM)] + [vmem] * 8,
        out_specs=[vmem] * 6,
        out_shape=[jax.ShapeDtypeStruct((HEADS, width), jnp.float32)] * 2
        + [jax.ShapeDtypeStruct((agents, width), jnp.bfloat16)] * 2
        + [jax.ShapeDtypeStruct((agents, width), jnp.float32)] * 2,
        scratch_shapes=[
            pltpu.VMEM((4, half, lanes, BLOCK), jnp.float32),
            pltpu.VMEM((cols, agents, BLOCK), jnp.bfloat16),
            pltpu.VMEM((cols, agents, BLOCK), jnp.bfloat16),
            pltpu.VMEM((cols, agents, BLOCK), jnp.float32),
            pltpu.VMEM((cols, lanes, BLOCK), jnp.bfloat16),
        ],
        compiler_params=pltpu.CompilerParams(vmem_limit_bytes=VMEM_LIMIT),
    )(rows, obs, keep, side, terms_own, rec_own, head_own, head_other, other)


def swap(v):
    return lax.ppermute(v, "blk", [(0, 1), (1, 0)])


def sum_over(v, axes):
    for axis in axes:
        size = lax.axis_size(axis)
        came = [
            lax.ppermute(v, axis, [(i, (i + k) % size) for i in range(size)])
            for k in range(1, size)
        ]
        v = sum(came, v)
    return v


def shards(
    observations,
    in_weight,
    rec_blocks,
    block_rows,
    episode_start,
    actions,
    rewards,
    mu_logp,
    head_weight,
    learner_of,
):
    blk = lax.axis_index("blk")
    num_agents, num_steps, obs_width = observations.shape
    mine = num_agents // 2
    cols = rec_blocks.shape[1]
    num_rep = 4 * cols
    rep = lax.axis_index(("x", "z", "core"))
    gate, col = rep // cols, rep % cols
    in_part = lax.dynamic_slice(in_weight, (0, gate, col * BLOCK), (obs_width, 1, BLOCK))
    rec_part = lax.dynamic_slice(
        rec_blocks, (gate, col, 0, 0, 0), (1, 1) + rec_blocks.shape[2:]
    )
    packed = jnp.concatenate(
        [in_part.reshape(-1, BLOCK), rec_part.reshape(-1, BLOCK)], axis=0
    )
    other = lax.all_gather(swap(packed), ("x", "z", "core"))

    head_own = jnp.pad(head_weight.T, ((0, HEAD_ROWS - head_weight.shape[1]), (0, 0)))
    head_other = swap(head_own)
    rows = jnp.concatenate([block_rows, swap(block_rows)], axis=1)
    rows = ((rows + cols * blk) % (2 * cols)).reshape(-1)

    onehot = (
        learner_of[:, 0][:, None] == jnp.arange(num_rep, dtype=jnp.int32)
    ).astype(jnp.float32)
    counts = sum_over(jnp.sum(onehot, axis=0), ("x", "z", "core"))
    agent_count = jnp.sum(onehot * counts[None, :], axis=1)
    weight = 1.0 / (jnp.maximum(agent_count, 1.0) * num_steps)

    starts = episode_start.astype(jnp.float32)
    next_start = jnp.concatenate([starts[:, 1:], jnp.zeros_like(starts[:, :1])], axis=1)
    side = jnp.stack(
        [
            rewards,
            mu_logp,
            actions.astype(jnp.float32),
            next_start,
            jnp.broadcast_to(weight[:, None], rewards.shape),
        ]
        + [jnp.zeros_like(rewards)] * 3
    )
    side = lax.dynamic_slice_in_dim(side, blk * mine, mine, 1)
    side = jnp.swapaxes(side, 1, 2).reshape(8, num_steps * mine)
    keep = 1.0 - lax.dynamic_slice_in_dim(starts, blk * mine, mine, 0).T[:, :, None]
    obs = lax.dynamic_slice_in_dim(observations, blk * mine, mine, 0)
    obs = jnp.swapaxes(obs, 0, 1).reshape(num_steps * mine, obs_width)

    terms_own = input_terms(obs, in_weight)

    grad_own, grad_other, hidden_own, hidden_other, cell_own, cell_other = rollout(
        rows, obs, keep, side, terms_own, rec_blocks, head_own, head_other, other
    )
    grad = sum_over(grad_own + swap(grad_other), TORUS)
    head_grad = grad[: head_weight.shape[1]].T

    def place(here, there):
        first = jnp.where(blk == 0, here, there)
        second = jnp.where(blk == 0, there, here)
        return jnp.concatenate([first, second], axis=0)

    hidden_last = place(hidden_own, swap(hidden_other))
    cell_last = place(cell_own, swap(cell_other))
    return (head_grad, hidden_last, cell_last)


def solution(mesh):
    fine = Mesh(mesh.devices.reshape(4, 4, 4, 2, 2), ("y", "x", "z", "core", "blk"))
    rows = TORUS
    return jax.shard_map(
        shards,
        mesh=fine,
        in_specs=(
            P(rows, None, None),
            P(None, None, "blk"),
            P(None, "blk", None, None, None),
            P(None, "blk", None),
            P(rows, None),
            P(rows, None),
            P(rows, None),
            P(rows, None),
            P("blk", None),
            P(rows, None),
        ),
        out_specs=(P("blk", None), P(rows, "blk"), P(rows, "blk")),
        check_vma=False,
    )
```

```python
import jax
import jax.numpy as jnp
from jax import lax
from jax.experimental import pallas as pl
from jax.experimental.pallas import tpu as pltpu
from jax.sharding import Mesh, PartitionSpec as P

GAMMA_RATE = 0.99
BLOCK = 128
HEADS = 24
HEAD_ROWS = 32
STEPS = 32
RING_PARTS = 8
CUT = 384
VMEM_LIMIT = 32 * 1024 * 1024
SMALL_LIMIT = 16 * 1024 * 1024
TORUS = ("y", "x", "z", "core")


def sigmoid(x):
    return 0.5 * jnp.tanh(0.5 * x) + 0.5


def input_kernel(obs_ref, weight_ref, out_ref):
    wide = 2 * BLOCK

    def body(i, _):
        for g in range(4):
            w = weight_ref[:, g, pl.ds(pl.multiple_of(i * wide, wide), wide)]
            out = jnp.dot(obs_ref[...], w, preferred_element_type=jnp.float32)
            for j in range(2):
                out_ref[g, 2 * i + j] = out[:, j * BLOCK : (j + 1) * BLOCK]
        return 0

    lax.fori_loop(0, weight_ref.shape[2] // wide, body, 0)


def input_terms(obs, weight):
    vmem = pl.BlockSpec(memory_space=pltpu.VMEM)
    return pl.pallas_call(
        input_kernel,
        in_specs=[vmem] * 2,
        out_specs=vmem,
        out_shape=jax.ShapeDtypeStruct(
            (4, weight.shape[2] // BLOCK, obs.shape[0], BLOCK), jnp.float32
        ),
        compiler_params=pltpu.CompilerParams(vmem_limit_bytes=SMALL_LIMIT),
    )(obs, weight)


def rollout_kernel(table_ref, obs_ref, keep_ref, terms_own_ref, rec_own_ref, *refs):
    parts_a, parts_b = refs[:RING_PARTS], refs[RING_PARTS : 2 * RING_PARTS]
    traj, hidden_own_ref, hidden_other_ref, cell_own_ref, cell_other_ref = refs[
        2 * RING_PARTS : 2 * RING_PARTS + 5
    ]
    terms_other, other_ref, state_a, state_b, cell, sems = refs[2 * RING_PARTS + 5 :]
    steps, agents, _ = keep_ref.shape
    cols = traj.shape[0]
    half = cols // 2
    lanes = steps * agents
    obs_width = obs_ref.shape[1]
    rec_rows = 4 * BLOCK
    rows_ref = table_ref
    copies = []
    for parts, first in ((parts_a, 0), (parts_b, CUT)):
        for part in parts:
            for k in range(part.shape[0]):
                n = len(copies)
                to = table_ref[16 * cols + n]
                copies.append(
                    pltpu.make_async_copy(
                        part.at[k], other_ref.at[to, pl.ds(first, part.shape[1])], sems.at[n]
                    )
                )
    for copy in copies:
        copy.start()
    for copy in copies[: len(copies) // 2]:
        copy.wait()

    def in_other(i, _):
        for g in range(4):
            w = jnp.concatenate(
                [other_ref[g * half + 2 * i + j, :obs_width, :] for j in range(2)], axis=1
            )
            out = jnp.dot(obs_ref[...], w, preferred_element_type=jnp.float32)
            for j in range(2):
                terms_other[g, 2 * i + j] = out[:, j * BLOCK : (j + 1) * BLOCK]
        return 0

    lax.fori_loop(0, half // 2, in_other, 0)
    for copy in copies[len(copies) // 2 :]:
        copy.wait()

    state_a[...] = jnp.zeros_like(state_a)
    cell[...] = jnp.zeros_like(cell)

    def step(t, state, state_next):
        base = pl.multiple_of(t * agents, agents)
        keep = keep_ref[jnp.minimum(t + 1, steps - 1)]
        for c in range(cols):
            own, cc = c < half, c % half
            terms_ref = terms_own_ref if own else terms_other
            cell_ref = cell_own_ref if own else cell_other_ref
            pre = []
            for g in range(4):
                parts = [state[rows_ref[(g * cols + c) * 4 + k]] for k in range(4)]
                lhs = jnp.concatenate(parts, axis=1)
                if own:
                    rhs = rec_own_ref[g, cc].reshape(rec_rows, BLOCK)
                else:
                    rhs = other_ref[g * half + cc, obs_width:, :]
                pre.append(
                    terms_ref[g, cc, pl.ds(base, agents), :]
                    + jnp.dot(lhs, rhs, preferred_element_type=jnp.float32)
                )
            new_cell = sigmoid(pre[1]) * cell[c] + sigmoid(pre[0]) * jnp.tanh(pre[2])
            new_hidden = (sigmoid(pre[3]) * jnp.tanh(new_cell)).astype(jnp.bfloat16)
            traj[c, pl.ds(base, agents), :] = new_hidden
            state_next[c] = (new_hidden * keep).astype(jnp.bfloat16)
            cell_ref[:, cc * BLOCK : (cc + 1) * BLOCK] = new_cell
            cell[c] = new_cell * keep

    def two_steps(i, _):
        step(2 * i, state_a, state_b)
        step(2 * i + 1, state_b, state_a)
        return 0

    lax.fori_loop(0, steps // 2, two_steps, 0)
    for c in range(cols):
        cc = c % half
        hidden_ref = hidden_own_ref if c < half else hidden_other_ref
        hidden_ref[:, cc * BLOCK : (cc + 1) * BLOCK] = traj[c, lanes - agents :, :]


def head_kernel(
    traj, head_own_ref, head_other_ref, side_ref, grad_own_ref, grad_other_ref
):
    cols, lanes, _ = traj.shape
    half = cols // 2
    agents = lanes // STEPS
    out = jnp.zeros((HEAD_ROWS, lanes), jnp.float32)
    for c in range(cols):
        head_ref, cc = (head_own_ref if c < half else head_other_ref), c % half
        out = out + lax.dot_general(
            head_ref[:, cc * BLOCK : (cc + 1) * BLOCK],
            traj[c],
            (((1,), (1,)), ((), ())),
            preferred_element_type=jnp.float32,
        )
    logits = out[:16]
    value = out[16:17]
    side = side_ref[...]
    rewards, mu_logp, actions, next_start, weight = [side[i : i + 1] for i in range(5)]
    top = jnp.max(logits, axis=0, keepdims=True)
    shifted = jnp.exp(logits - top)
    total = jnp.sum(shifted, axis=0, keepdims=True)
    probs = shifted / total
    log_total = jnp.log(total) + top
    which = lax.broadcasted_iota(jnp.int32, logits.shape, 0).astype(jnp.float32)
    picked = (which == actions).astype(jnp.float32)
    logp = jnp.sum(picked * logits, axis=0, keepdims=True) - log_total
    rho = jnp.minimum(1.0, jnp.exp(logp - mu_logp))
    discount = GAMMA_RATE * (1.0 - next_start)
    lane = lax.broadcasted_iota(jnp.int32, value.shape, 1)
    last = lane >= lanes - agents

    def ahead(x, by):
        return pltpu.roll(x, lanes - by, 1)

    value_next = jnp.where(last, value, ahead(value, agents))
    acc = rho * (rewards + discount * value_next - value)
    factor = discount * rho
    by = agents
    while by < lanes:
        out_of = lane >= lanes - by
        acc = acc + factor * jnp.where(out_of, 0.0, ahead(acc, by))
        factor = factor * jnp.where(out_of, 0.0, ahead(factor, by))
        by *= 2
    targets = value + acc
    target_next = jnp.where(last, value, ahead(targets, agents))
    advantage = rho * (rewards + discount * target_next - value)
    d_logits = -(weight * advantage) * (picked - probs)
    d_value = weight * (value - targets)
    row = lax.broadcasted_iota(jnp.int32, (8, lanes), 0)
    d_tail = jnp.where(row == 0, d_value, 0.0)
    cot = jnp.concatenate([d_logits, d_tail], axis=0).astype(jnp.bfloat16)
    for c in range(cols):
        grad_ref, cc = (grad_own_ref if c < half else grad_other_ref), c % half
        grad_ref[:, cc * BLOCK : (cc + 1) * BLOCK] = jnp.dot(
            cot, traj[c], preferred_element_type=jnp.float32
        )


def rollout(table, obs, keep, terms_own, rec_own, parts_a, parts_b):
    steps, agents, _ = keep.shape
    half = rec_own.shape[1]
    cols, width, lanes = 2 * half, half * BLOCK, steps * agents
    vmem = pl.BlockSpec(memory_space=pltpu.VMEM)
    parts = list(parts_a) + list(parts_b)
    return pl.pallas_call(
        rollout_kernel,
        in_specs=[pl.BlockSpec(memory_space=pltpu.SMEM)]
        + [vmem] * 4
        + [pl.BlockSpec(memory_space=pl.ANY)] * len(parts),
        out_specs=[vmem] * 5,
        out_shape=[jax.ShapeDtypeStruct((cols, lanes, BLOCK), jnp.bfloat16)]
        + [jax.ShapeDtypeStruct((agents, width), jnp.bfloat16)] * 2
        + [jax.ShapeDtypeStruct((agents, width), jnp.float32)] * 2,
        scratch_shapes=[
            pltpu.VMEM((4, half, lanes, BLOCK), jnp.float32),
            pltpu.VMEM((4 * half, obs.shape[1] + 4 * BLOCK, BLOCK), jnp.bfloat16),
            pltpu.VMEM((cols, agents, BLOCK), jnp.bfloat16),
            pltpu.VMEM((cols, agents, BLOCK), jnp.bfloat16),
            pltpu.VMEM((cols, agents, BLOCK), jnp.float32),
            pltpu.SemaphoreType.DMA((8 * half,)),
        ],
        compiler_params=pltpu.CompilerParams(vmem_limit_bytes=VMEM_LIMIT),
    )(table, obs, keep, terms_own, rec_own, *parts)


def head_grads(traj, head_own, head_other, side):
    vmem = pl.BlockSpec(memory_space=pltpu.VMEM)
    width = traj.shape[0] // 2 * BLOCK
    return pl.pallas_call(
        head_kernel,
        in_specs=[vmem] * 4,
        out_specs=[vmem] * 2,
        out_shape=[jax.ShapeDtypeStruct((HEADS, width), jnp.float32)] * 2,
        compiler_params=pltpu.CompilerParams(vmem_limit_bytes=SMALL_LIMIT),
    )(traj, head_own, head_other, side)


def swap(v, axis="blk"):
    return lax.ppermute(v, axis, [(0, 1), (1, 0)])


def ring(v, axis):
    size = lax.axis_size(axis)
    return [v] + [
        lax.ppermute(v, axis, [(i, (i + k) % size) for i in range(size)])
        for k in range(1, size)
    ]


def sum_over(v, axes):
    for axis in axes:
        v = sum(ring(v, axis)[1:], v)
    return v


def shards(
    observations,
    in_weight,
    rec_blocks,
    block_rows,
    episode_start,
    actions,
    rewards,
    mu_logp,
    head_weight,
    learner_of,
):
    blk = lax.axis_index("blk")
    num_agents, num_steps, obs_width = observations.shape
    mine = num_agents // 2
    cols = rec_blocks.shape[1]
    num_rep = 4 * cols
    place_y, place_x, place_core = [lax.axis_index(a) for a in ("y", "x", "core")]
    gate, col = place_y, 2 * place_x + place_core
    in_part = lax.dynamic_slice(in_weight, (0, gate, col * BLOCK), (obs_width, 1, BLOCK))
    rec_part = lax.dynamic_slice(
        rec_blocks, (gate, col, 0, 0, 0), (1, 1) + rec_blocks.shape[2:]
    )
    packed = jnp.concatenate(
        [in_part.reshape(-1, BLOCK), rec_part.reshape(-1, BLOCK)], axis=0
    )
    packed, learner_of = lax.optimization_barrier((packed, learner_of))
    packed = swap(packed)
    rows_other = swap(block_rows)
    onehot = (
        learner_of[:, 0][:, None] == jnp.arange(num_rep, dtype=jnp.int32)
    ).astype(jnp.float32)
    counts = sum_over(jnp.sum(onehot, axis=0), ("x", "z", "core"))
    packed, rows_other, counts = lax.optimization_barrier((packed, rows_other, counts))
    over_x = ring(packed[:CUT], "x")
    over_y = ring(packed[CUT:], "y")
    head_own = jnp.pad(head_weight.T, ((0, HEAD_ROWS - head_weight.shape[1]), (0, 0)))
    over_x, over_y, head_own = lax.optimization_barrier(
        (jnp.stack(over_x), jnp.stack(over_y), head_own)
    )
    head_other = swap(head_own)
    parts_a, parts_b = ring(over_x, "y"), ring(over_y, "x")
    parts_a, parts_b, head_other = lax.optimization_barrier((parts_a, parts_b, head_other))
    parts_a = parts_a + [swap(p, "core") for p in parts_a]
    parts_b = parts_b + [swap(p, "core") for p in parts_b]
    back = jnp.arange(4, dtype=jnp.int32)
    from_y, from_x = (place_y - back) % 4, (place_x - back) % 4
    from_core = jnp.stack([place_core, 1 - place_core])
    index = (
        8 * from_y[None, :, None] + 2 * from_x[None, None, :] + from_core[:, None, None]
    )
    index = jnp.concatenate([index.reshape(-1), jnp.swapaxes(index, 1, 2).reshape(-1)])

    rows = jnp.concatenate([block_rows, rows_other], axis=1)
    rows = ((rows + cols * blk) % (2 * cols)).reshape(-1)
    table = jnp.concatenate([rows, index.astype(jnp.int32)])

    agent_count = jnp.sum(onehot * counts[None, :], axis=1)
    weight = 1.0 / (jnp.maximum(agent_count, 1.0) * num_steps)

    starts = episode_start.astype(jnp.float32)
    next_start = jnp.concatenate([starts[:, 1:], jnp.zeros_like(starts[:, :1])], axis=1)
    side = jnp.stack(
        [
            rewards,
            mu_logp,
            actions.astype(jnp.float32),
            next_start,
            jnp.broadcast_to(weight[:, None], rewards.shape),
        ]
        + [jnp.zeros_like(rewards)] * 3
    )
    side = lax.dynamic_slice_in_dim(side, blk * mine, mine, 1)
    side = jnp.swapaxes(side, 1, 2).reshape(8, num_steps * mine)
    keep = 1.0 - lax.dynamic_slice_in_dim(starts, blk * mine, mine, 0).T[:, :, None]
    obs = lax.dynamic_slice_in_dim(observations, blk * mine, mine, 0)
    obs = jnp.swapaxes(obs, 0, 1).reshape(num_steps * mine, obs_width)

    terms_own = input_terms(obs, in_weight)

    traj, hidden_own, hidden_other, cell_own, cell_other = rollout(
        table, obs, keep, terms_own, rec_blocks, parts_a, parts_b
    )
    grad_own, grad_other = head_grads(traj, head_own, head_other, side)
    grad = sum_over(grad_own + swap(grad_other), TORUS)
    head_grad = grad[: head_weight.shape[1]].T

    def place(here, there):
        first = jnp.where(blk == 0, here, there)
        second = jnp.where(blk == 0, there, here)
        return jnp.concatenate([first, second], axis=0)

    hidden_last = place(hidden_own, swap(hidden_other))
    cell_last = place(cell_own, swap(cell_other))
    return (head_grad, hidden_last, cell_last)


def solution(mesh):
    fine = Mesh(mesh.devices.reshape(4, 4, 4, 2, 2), ("y", "x", "z", "core", "blk"))
    rows = TORUS
    return jax.shard_map(
        shards,
        mesh=fine,
        in_specs=(
            P(rows, None, None),
            P(None, None, "blk"),
            P(None, "blk", None, None, None),
            P(None, "blk", None),
            P(rows, None),
            P(rows, None),
            P(rows, None),
            P(rows, None),
            P("blk", None),
            P(rows, None),
        ),
        out_specs=(P("blk", None), P(rows, "blk"), P(rows, "blk")),
        check_vma=False,
    )
```

```python
import jax
import jax.numpy as jnp
from jax import lax
from jax.experimental import pallas as pl
from jax.experimental.pallas import tpu as pltpu
from jax.sharding import Mesh, PartitionSpec as P

GAMMA_RATE = 0.99
BLOCK = 128
HEADS = 24
HEAD_ROWS = 32
STEPS = 32
RING_PARTS = 8
CUT = 384
PAD = 16
NUM_HEADS = 17
GRAD_ROWS = 72
VMEM_LIMIT = 32 * 1024 * 1024
SMALL_LIMIT = 16 * 1024 * 1024
TORUS = ("y", "x", "z", "core")


def sigmoid(x):
    return 0.5 * jnp.tanh(0.5 * x) + 0.5


def input_kernel(obs_ref, weight_ref, out_ref):
    wide = 2 * BLOCK

    def body(i, _):
        for g in range(4):
            w = weight_ref[:, g, pl.ds(pl.multiple_of(i * wide, wide), wide)]
            out = jnp.dot(obs_ref[...], w, preferred_element_type=jnp.float32)
            for j in range(2):
                out_ref[g, 2 * i + j] = out[:, j * BLOCK : (j + 1) * BLOCK]
        return 0

    lax.fori_loop(0, weight_ref.shape[2] // wide, body, 0)


def input_terms(obs, weight):
    vmem = pl.BlockSpec(memory_space=pltpu.VMEM)
    return pl.pallas_call(
        input_kernel,
        in_specs=[vmem] * 2,
        out_specs=vmem,
        out_shape=jax.ShapeDtypeStruct(
            (4, weight.shape[2] // BLOCK, obs.shape[0], BLOCK), jnp.float32
        ),
        compiler_params=pltpu.CompilerParams(vmem_limit_bytes=SMALL_LIMIT),
    )(obs, weight)


def rollout_kernel(
    table_ref, rows_own_ref, rows_other_ref, obs_ref, keep_ref, terms_own_ref, rec_hbm, *refs
):
    parts_a, parts_b = refs[:RING_PARTS], refs[RING_PARTS : 2 * RING_PARTS]
    traj, hidden_own_ref, cell_own_ref, states_ref, counts_ref = refs[
        2 * RING_PARTS : 2 * RING_PARTS + 5
    ]
    terms_other, other_ref, rec_own_ref, told, state_a, state_b, cell, sems = refs[
        2 * RING_PARTS + 5 :
    ]
    steps, agents, _ = keep_ref.shape
    cols = traj.shape[0]
    half = cols // 2
    lanes = steps * agents
    obs_width = obs_ref.shape[1]
    rec_rows = 4 * BLOCK
    size = 2 * half * 2
    own_at = table_ref[2 * size]
    other_at = half - own_at
    copies = []
    for parts, first in ((parts_a, 0), (parts_b, CUT)):
        for part in parts:
            for k in range(4):
                n = len(copies)
                copies.append(
                    pltpu.make_async_copy(
                        part.at[pl.ds(k * CUT, CUT)],
                        other_ref.at[table_ref[n], pl.ds(first, CUT)],
                        sems.at[n],
                    )
                )
    for i, part in enumerate(parts_b):
        copies.append(
            pltpu.make_async_copy(
                part.at[pl.ds(4 * CUT, PAD)], told.at[i], sems.at[len(copies)]
            )
        )
    copies.append(pltpu.make_async_copy(rec_hbm, rec_own_ref, sems.at[len(copies)]))
    for copy in copies:
        copy.start()
    for copy in copies[:size]:
        copy.wait()

    def in_other(i, _):
        for g in range(4):
            w = jnp.concatenate(
                [other_ref[g * half + 2 * i + j, :obs_width, :] for j in range(2)], axis=1
            )
            out = jnp.dot(obs_ref[...], w, preferred_element_type=jnp.float32)
            for j in range(2):
                terms_other[g, 2 * i + j] = out[:, j * BLOCK : (j + 1) * BLOCK]
        return 0

    lax.fori_loop(0, half // 2, in_other, 0)
    for copy in copies[size:]:
        copy.wait()
    counts_ref[...] = sum([told[i].astype(jnp.float32) for i in range(RING_PARTS)])

    state_a[...] = jnp.zeros_like(state_a)
    cell[...] = jnp.zeros_like(cell)

    def step(t, state, state_next):
        base = pl.multiple_of(t * agents, agents)
        keep = keep_ref[jnp.minimum(t + 1, steps - 1)]
        for c in range(cols):
            own, cc = c < half, c % half
            terms_ref = terms_own_ref if own else terms_other
            rows_ref = rows_own_ref if own else rows_other_ref
            at = (own_at if own else other_at) + cc
            pre = []
            for g in range(4):
                parts = [state[rows_ref[(g * half + cc) * 4 + k]] for k in range(4)]
                lhs = jnp.concatenate(parts, axis=1)
                if own:
                    rhs = rec_own_ref[g, cc].reshape(rec_rows, BLOCK)
                else:
                    rhs = other_ref[g * half + cc, obs_width:, :]
                pre.append(
                    terms_ref[g, cc, pl.ds(base, agents), :]
                    + jnp.dot(lhs, rhs, preferred_element_type=jnp.float32)
                )
            new_cell = sigmoid(pre[1]) * cell[c] + sigmoid(pre[0]) * jnp.tanh(pre[2])
            new_hidden = (sigmoid(pre[3]) * jnp.tanh(new_cell)).astype(jnp.bfloat16)
            traj[c, pl.ds(base, agents), :] = new_hidden
            state_next[at] = (new_hidden * keep).astype(jnp.bfloat16)
            block = slice(cc * BLOCK, (cc + 1) * BLOCK)
            if own:
                cell_own_ref[:, block] = new_cell
            else:
                states_ref[:agents, block] = new_cell
            cell[c] = new_cell * keep

    def two_steps(i, _):
        step(2 * i, state_a, state_b)
        step(2 * i + 1, state_b, state_a)
        return 0

    lax.fori_loop(0, steps // 2, two_steps, 0)
    for c in range(half):
        block = slice(c * BLOCK, (c + 1) * BLOCK)
        hidden_own_ref[:, block] = traj[c, lanes - agents :, :]
        states_ref[agents:, block] = traj[half + c, lanes - agents :, :].astype(jnp.float32)


def head_kernel(
    place_ref, traj, head_own_ref, head_other_ref, side_ref, counts_ref, keep_ref, send_ref
):
    cols, lanes, _ = traj.shape
    half = cols // 2
    agents = lanes // STEPS
    out = jnp.zeros((HEAD_ROWS, lanes), jnp.float32)
    for c in range(cols):
        head_ref, cc = (head_own_ref if c < half else head_other_ref), c % half
        out = out + lax.dot_general(
            head_ref[:, cc * BLOCK : (cc + 1) * BLOCK],
            traj[c],
            (((1,), (1,)), ((), ())),
            preferred_element_type=jnp.float32,
        )
    logits = out[:16]
    value = out[16:17]
    side = side_ref[...]
    rewards, mu_logp, actions, next_start, learner = [side[i : i + 1] for i in range(5)]
    named = lax.broadcasted_iota(jnp.int32, (BLOCK, lanes), 0).astype(jnp.float32) == learner
    count = jnp.dot(
        counts_ref[...].astype(jnp.bfloat16),
        named.astype(jnp.bfloat16),
        preferred_element_type=jnp.float32,
    )[:1]
    weight = 1.0 / (jnp.maximum(count, 1.0) * STEPS)
    top = jnp.max(logits, axis=0, keepdims=True)
    shifted = jnp.exp(logits - top)
    total = jnp.sum(shifted, axis=0, keepdims=True)
    probs = shifted / total
    log_total = jnp.log(total) + top
    which = lax.broadcasted_iota(jnp.int32, logits.shape, 0).astype(jnp.float32)
    picked = (which == actions).astype(jnp.float32)
    logp = jnp.sum(picked * logits, axis=0, keepdims=True) - log_total
    rho = jnp.minimum(1.0, jnp.exp(logp - mu_logp))
    discount = GAMMA_RATE * (1.0 - next_start)
    lane = lax.broadcasted_iota(jnp.int32, value.shape, 1)
    last = lane >= lanes - agents

    def ahead(x, by):
        return pltpu.roll(x, lanes - by, 1)

    value_next = jnp.where(last, value, ahead(value, agents))
    acc = rho * (rewards + discount * value_next - value)
    factor = discount * rho
    by = agents
    while by < lanes:
        out_of = lane >= lanes - by
        acc = acc + factor * jnp.where(out_of, 0.0, ahead(acc, by))
        factor = factor * jnp.where(out_of, 0.0, ahead(factor, by))
        by *= 2
    targets = value + acc
    target_next = jnp.where(last, value, ahead(targets, agents))
    advantage = rho * (rewards + discount * target_next - value)
    d_logits = -(weight * advantage) * (picked - probs)
    d_value = weight * (value - targets)
    row = lax.broadcasted_iota(jnp.int32, (8, lanes), 0)
    d_tail = jnp.where(row == 0, d_value, 0.0)
    cot = jnp.concatenate([d_logits, d_tail], axis=0).astype(jnp.bfloat16)
    zeros = jnp.zeros((GRAD_ROWS, BLOCK), jnp.float32)
    for side_of in range(2):
        keep_ref[side_of] = zeros
        send_ref[side_of] = zeros
    core = place_ref[0]
    quarter = half // 2
    for side_of in range(2):
        for j in range(quarter):
            rows = slice(j * NUM_HEADS, (j + 1) * NUM_HEADS)
            for ref, who in ((keep_ref, core), (send_ref, 1 - core)):
                part = traj[side_of * half + who * quarter + j]
                out = jnp.dot(cot, part, preferred_element_type=jnp.float32)
                ref[side_of, rows, :] = out[:NUM_HEADS]


def rollout(table, rows_own, rows_other, obs, keep, terms_own, rec_own, parts_a, parts_b):
    steps, agents, _ = keep.shape
    half = rec_own.shape[1]
    cols, width, lanes = 2 * half, half * BLOCK, steps * agents
    vmem, smem, anywhere = [
        pl.BlockSpec(memory_space=m) for m in (pltpu.VMEM, pltpu.SMEM, pl.ANY)
    ]
    parts = list(parts_a) + list(parts_b)
    return pl.pallas_call(
        rollout_kernel,
        in_specs=[smem] * 3 + [vmem] * 3 + [anywhere] * (1 + len(parts)),
        out_specs=[vmem] * 5,
        out_shape=[
            jax.ShapeDtypeStruct((cols, lanes, BLOCK), jnp.bfloat16),
            jax.ShapeDtypeStruct((agents, width), jnp.bfloat16),
            jax.ShapeDtypeStruct((agents, width), jnp.float32),
            jax.ShapeDtypeStruct((2 * agents, width), jnp.float32),
            jax.ShapeDtypeStruct((PAD, BLOCK), jnp.float32),
        ],
        scratch_shapes=[
            pltpu.VMEM((4, half, lanes, BLOCK), jnp.float32),
            pltpu.VMEM((4 * half, 2 * CUT, BLOCK), jnp.bfloat16),
            pltpu.VMEM(rec_own.shape, jnp.bfloat16),
            pltpu.VMEM((RING_PARTS, PAD, BLOCK), jnp.bfloat16),
            pltpu.VMEM((cols, agents, BLOCK), jnp.bfloat16),
            pltpu.VMEM((cols, agents, BLOCK), jnp.bfloat16),
            pltpu.VMEM((cols, agents, BLOCK), jnp.float32),
            pltpu.SemaphoreType.DMA((8 * half + RING_PARTS + 1,)),
        ],
        compiler_params=pltpu.CompilerParams(vmem_limit_bytes=VMEM_LIMIT),
    )(table, rows_own, rows_other, obs, keep, terms_own, rec_own, *parts)


def head_grads(place, traj, head_own, head_other, side, counts):
    vmem = pl.BlockSpec(memory_space=pltpu.VMEM)
    return pl.pallas_call(
        head_kernel,
        in_specs=[pl.BlockSpec(memory_space=pltpu.SMEM)] + [vmem] * 5,
        out_specs=[vmem] * 2,
        out_shape=[jax.ShapeDtypeStruct((2, GRAD_ROWS, BLOCK), jnp.float32)] * 2,
        compiler_params=pltpu.CompilerParams(vmem_limit_bytes=SMALL_LIMIT),
    )(place, traj, head_own, head_other, side, counts)


def swap(v, axis="blk"):
    return lax.ppermute(v, axis, [(0, 1), (1, 0)])


def ring(v, axis):
    size = lax.axis_size(axis)
    return [v] + [
        lax.ppermute(v, axis, [(i, (i + k) % size) for i in range(size)])
        for k in range(1, size)
    ]


def sum_over(v, axes):
    for axis in axes:
        v = sum(ring(v, axis)[1:], v)
    return v


def shards(
    observations,
    in_weight,
    rec_blocks,
    block_rows,
    episode_start,
    actions,
    rewards,
    mu_logp,
    head_weight,
    learner_of,
):
    blk = lax.axis_index("blk")
    num_agents, num_steps, obs_width = observations.shape
    mine = num_agents // 2
    cols = rec_blocks.shape[1]
    place_y, place_x, place_core = [lax.axis_index(a) for a in ("y", "x", "core")]
    gate, col = place_y, 2 * place_x + place_core
    in_part = lax.dynamic_slice(in_weight, (0, gate, col * BLOCK), (obs_width, 1, BLOCK))
    rec_part = lax.dynamic_slice(
        rec_blocks, (gate, col, 0, 0, 0), (1, 1) + rec_blocks.shape[2:]
    )
    packed = jnp.concatenate(
        [in_part.reshape(-1, BLOCK), rec_part.reshape(-1, BLOCK)], axis=0
    )
    head_own = jnp.pad(head_weight.T, ((0, HEAD_ROWS - head_weight.shape[1]), (0, 0)))
    head_other = swap(head_own)
    rows_own = block_rows.reshape(-1)
    rows_other = swap(rows_own)
    packed, learner = lax.optimization_barrier((swap(packed), learner_of))

    over_x = ring(packed[:CUT], "x")
    over_y = ring(packed[CUT:], "y")
    onehot = learner == jnp.arange(BLOCK, dtype=jnp.int32)[None, :]
    counts = jnp.sum(onehot.astype(jnp.bfloat16), axis=0, keepdims=True)
    counts = sum_over(jnp.broadcast_to(counts, (PAD, BLOCK)), ("z",))
    over_x = jnp.concatenate(over_x, axis=0)
    over_y = jnp.concatenate(over_y + [counts], axis=0)

    back = jnp.arange(4, dtype=jnp.int32)
    from_y, from_x = (place_y - back) % 4, (place_x - back) % 4
    from_core = jnp.stack([place_core, 1 - place_core])
    index = (
        8 * from_y[None, :, None] + 2 * from_x[None, None, :] + from_core[:, None, None]
    )
    table = jnp.concatenate(
        [index.reshape(-1), jnp.swapaxes(index, 1, 2).reshape(-1), (cols * blk).reshape(1)]
    ).astype(jnp.int32)

    starts = episode_start.astype(jnp.float32)
    next_start = jnp.concatenate([starts[:, 1:], jnp.zeros_like(starts[:, :1])], axis=1)
    side = jnp.stack(
        [
            rewards,
            mu_logp,
            actions.astype(jnp.float32),
            next_start,
            jnp.broadcast_to(learner_of.astype(jnp.float32), rewards.shape),
        ]
        + [jnp.zeros_like(rewards)] * 3
    )
    side = lax.dynamic_slice_in_dim(side, blk * mine, mine, 1)
    side = jnp.swapaxes(side, 1, 2).reshape(8, num_steps * mine)
    keep = 1.0 - lax.dynamic_slice_in_dim(starts, blk * mine, mine, 0).T[:, :, None]
    obs = lax.dynamic_slice_in_dim(observations, blk * mine, mine, 0)
    obs = jnp.swapaxes(obs, 0, 1).reshape(num_steps * mine, obs_width)

    over_x, over_y, obs, keep, side, table, rows_own, rows_other = lax.optimization_barrier(
        (over_x, over_y, obs, keep, side, table, rows_own, rows_other)
    )
    parts_a, parts_b = ring(over_x, "y"), ring(over_y, "x")
    terms_own = input_terms(obs, in_weight)
    parts_a, parts_b = lax.optimization_barrier((parts_a, parts_b))
    parts_a = parts_a + [swap(p, "core") for p in parts_a]
    parts_b = parts_b + [swap(p, "core") for p in parts_b]

    traj, hidden_own, cell_own, states, counts = rollout(
        table, rows_own, rows_other, obs, keep, terms_own, rec_blocks, parts_a, parts_b
    )
    mate = place_core.reshape(1).astype(jnp.int32)
    kept, sent = head_grads(mate, traj, head_own, head_other, side, counts)
    kept = kept + swap(sent, "core")
    grad = kept[0] + swap(kept[1])
    grad, states = lax.optimization_barrier((sum_over(grad, ("y",)), states))
    states = swap(states)
    grad = sum_over(grad, ("x", "z"))
    grad_mate = swap(grad, "core")
    quarters = [jnp.where(place_core == i, grad, grad_mate) for i in range(2)]
    head_grad = jnp.concatenate(
        [
            q[j * NUM_HEADS : (j + 1) * NUM_HEADS]
            for q in quarters
            for j in range(cols // 2)
        ],
        axis=1,
    ).T

    def place(here, there):
        first = jnp.where(blk == 0, here, there)
        second = jnp.where(blk == 0, there, here)
        return jnp.concatenate([first, second], axis=0)

    cell_last = place(cell_own, states[:mine])
    hidden_last = place(hidden_own, states[mine:].astype(jnp.bfloat16))
    return (head_grad, hidden_last, cell_last)


def solution(mesh):
    fine = Mesh(mesh.devices.reshape(4, 4, 4, 2, 2), ("y", "x", "z", "core", "blk"))
    rows = TORUS
    return jax.shard_map(
        shards,
        mesh=fine,
        in_specs=(
            P(rows, None, None),
            P(None, None, "blk"),
            P(None, "blk", None, None, None),
            P(None, "blk", None),
            P(rows, None),
            P(rows, None),
            P(rows, None),
            P(rows, None),
            P("blk", None),
            P(rows, None),
        ),
        out_specs=(P("blk", None), P(rows, "blk"), P(rows, "blk")),
        check_vma=False,
    )
```

```python
import jax
import jax.numpy as jnp
from jax import lax
from jax.experimental import pallas as pl
from jax.experimental.pallas import tpu as pltpu
from jax.sharding import Mesh, PartitionSpec as P

GAMMA_RATE = 0.99
BLOCK = 128
HEADS = 24
HEAD_ROWS = 32
STEPS = 32
RING_PARTS = 8
CUT = 384
COUNT_ROWS = 64
NUM_HEADS = 17
GRAD_ROWS = 72
VMEM_LIMIT = 32 * 1024 * 1024
SMALL_LIMIT = 16 * 1024 * 1024
TORUS = ("y", "x", "z", "core")


def sigmoid(x):
    return 0.5 * jnp.tanh(0.5 * x) + 0.5


def input_kernel(obs_ref, weight_ref, out_ref):
    wide = 2 * BLOCK

    def body(i, _):
        for g in range(4):
            w = weight_ref[:, g, pl.ds(pl.multiple_of(i * wide, wide), wide)]
            out = jnp.dot(obs_ref[...], w, preferred_element_type=jnp.float32)
            for j in range(2):
                out_ref[g, 2 * i + j] = out[:, j * BLOCK : (j + 1) * BLOCK]
        return 0

    lax.fori_loop(0, weight_ref.shape[2] // wide, body, 0)


def input_terms(obs, weight):
    vmem = pl.BlockSpec(memory_space=pltpu.VMEM)
    return pl.pallas_call(
        input_kernel,
        in_specs=[vmem] * 2,
        out_specs=vmem,
        out_shape=jax.ShapeDtypeStruct(
            (4, weight.shape[2] // BLOCK, obs.shape[0], BLOCK), jnp.float32
        ),
        compiler_params=pltpu.CompilerParams(vmem_limit_bytes=SMALL_LIMIT),
    )(obs, weight)


def rollout_kernel(
    table_ref, rows_own_ref, rows_other_ref, obs_ref, starts_ref, terms_own_ref, rec_hbm, *refs
):
    parts_a, parts_b = refs[:RING_PARTS], refs[RING_PARTS : 2 * RING_PARTS]
    traj, hidden_own_ref, cell_own_ref, states_ref = refs[
        2 * RING_PARTS : 2 * RING_PARTS + 4
    ]
    terms_other, other_ref, rec_own_ref, state_a, state_b, cell, sems = refs[
        2 * RING_PARTS + 4 :
    ]
    steps = starts_ref.shape[1]
    agents = starts_ref.shape[0] // 2
    cols = traj.shape[0]
    half = cols // 2
    lanes = steps * agents
    obs_width = obs_ref.shape[1]
    rec_rows = 4 * BLOCK
    size = 2 * half * 2
    own_at = table_ref[2 * size]
    other_at = half - own_at
    copies = []
    for parts, first in ((parts_a, 0), (parts_b, CUT)):
        for part in parts:
            for k in range(4):
                n = len(copies)
                copies.append(
                    pltpu.make_async_copy(
                        part.at[pl.ds(k * CUT, CUT)],
                        other_ref.at[table_ref[n], pl.ds(first, CUT)],
                        sems.at[n],
                    )
                )
    copies.append(pltpu.make_async_copy(rec_hbm, rec_own_ref, sems.at[len(copies)]))
    for copy in copies:
        copy.start()
    for copy in copies[:size]:
        copy.wait()

    def in_other(i, _):
        for g in range(4):
            w = jnp.concatenate(
                [other_ref[g * half + 2 * i + j, :obs_width, :] for j in range(2)], axis=1
            )
            out = jnp.dot(obs_ref[...], w, preferred_element_type=jnp.float32)
            for j in range(2):
                terms_other[g, 2 * i + j] = out[:, j * BLOCK : (j + 1) * BLOCK]
        return 0

    lax.fori_loop(0, half // 2, in_other, 0)
    for copy in copies[size:]:
        copy.wait()

    begins = starts_ref[pl.ds(pl.multiple_of(table_ref[2 * size + 1], agents), agents), :]
    begins = begins.astype(jnp.float32)
    lane = lax.broadcasted_iota(jnp.int32, begins.shape, 1)
    state_a[...] = jnp.zeros_like(state_a)
    cell[...] = jnp.zeros_like(cell)

    def step(t, state, state_next):
        base = pl.multiple_of(t * agents, agents)
        keep = 1.0 - jnp.sum(jnp.where(lane == t + 1, begins, 0.0), axis=1, keepdims=True)
        for c in range(cols):
            own, cc = c < half, c % half
            terms_ref = terms_own_ref if own else terms_other
            rows_ref = rows_own_ref if own else rows_other_ref
            at = (own_at if own else other_at) + cc
            pre = []
            for g in range(4):
                parts = [state[rows_ref[(g * half + cc) * 4 + k]] for k in range(4)]
                lhs = jnp.concatenate(parts, axis=1)
                if own:
                    rhs = rec_own_ref[g, cc].reshape(rec_rows, BLOCK)
                else:
                    rhs = other_ref[g * half + cc, obs_width:, :]
                pre.append(
                    terms_ref[g, cc, pl.ds(base, agents), :]
                    + jnp.dot(lhs, rhs, preferred_element_type=jnp.float32)
                )
            new_cell = sigmoid(pre[1]) * cell[c] + sigmoid(pre[0]) * jnp.tanh(pre[2])
            new_hidden = (sigmoid(pre[3]) * jnp.tanh(new_cell)).astype(jnp.bfloat16)
            traj[c, pl.ds(base, agents), :] = new_hidden
            state_next[at] = (new_hidden * keep).astype(jnp.bfloat16)
            block = slice(cc * BLOCK, (cc + 1) * BLOCK)
            if own:
                cell_own_ref[:, block] = new_cell
            else:
                states_ref[:agents, block] = new_cell
            cell[c] = new_cell * keep

    def two_steps(i, _):
        step(2 * i, state_a, state_b)
        step(2 * i + 1, state_b, state_a)
        return 0

    lax.fori_loop(0, steps // 2, two_steps, 0)
    for c in range(half):
        block = slice(c * BLOCK, (c + 1) * BLOCK)
        hidden_own_ref[:, block] = traj[c, lanes - agents :, :]
        states_ref[agents:, block] = traj[half + c, lanes - agents :, :].astype(jnp.float32)


def head_kernel(
    place_ref, traj, head_own_ref, head_other_ref, side_ref, counts_hbm, keep_ref, send_ref, told, sem
):
    cols, lanes, _ = traj.shape
    half = cols // 2
    agents = lanes // STEPS
    copy = pltpu.make_async_copy(counts_hbm.at[:, pl.ds(0, 8)], told, sem)
    copy.start()
    out = jnp.zeros((HEAD_ROWS, lanes), jnp.float32)
    for c in range(cols):
        head_ref, cc = (head_own_ref if c < half else head_other_ref), c % half
        out = out + lax.dot_general(
            head_ref[:, cc * BLOCK : (cc + 1) * BLOCK],
            traj[c],
            (((1,), (1,)), ((), ())),
            preferred_element_type=jnp.float32,
        )
    logits = out[:16]
    value = out[16:17]
    side = side_ref[...]
    rewards, mu_logp, actions, next_start, learner = [side[i : i + 1] for i in range(5)]
    named = lax.broadcasted_iota(jnp.int32, (BLOCK, lanes), 0).astype(jnp.float32) == learner
    copy.wait()
    counts = sum([told[i] for i in range(told.shape[0])])
    count = jnp.dot(
        counts.astype(jnp.bfloat16),
        named.astype(jnp.bfloat16),
        preferred_element_type=jnp.float32,
    )[:1]
    weight = 1.0 / (jnp.maximum(count, 1.0) * STEPS)
    top = jnp.max(logits, axis=0, keepdims=True)
    shifted = jnp.exp(logits - top)
    total = jnp.sum(shifted, axis=0, keepdims=True)
    probs = shifted / total
    log_total = jnp.log(total) + top
    which = lax.broadcasted_iota(jnp.int32, logits.shape, 0).astype(jnp.float32)
    picked = (which == actions).astype(jnp.float32)
    logp = jnp.sum(picked * logits, axis=0, keepdims=True) - log_total
    rho = jnp.minimum(1.0, jnp.exp(logp - mu_logp))
    discount = GAMMA_RATE * (1.0 - next_start)
    lane = lax.broadcasted_iota(jnp.int32, value.shape, 1)
    last = lane >= lanes - agents

    def ahead(x, by):
        return pltpu.roll(x, lanes - by, 1)

    value_next = jnp.where(last, value, ahead(value, agents))
    acc = rho * (rewards + discount * value_next - value)
    factor = discount * rho
    by = agents
    while by < lanes:
        out_of = lane >= lanes - by
        acc = acc + factor * jnp.where(out_of, 0.0, ahead(acc, by))
        factor = factor * jnp.where(out_of, 0.0, ahead(factor, by))
        by *= 2
    targets = value + acc
    target_next = jnp.where(last, value, ahead(targets, agents))
    advantage = rho * (rewards + discount * target_next - value)
    d_logits = -(weight * advantage) * (picked - probs)
    d_value = weight * (value - targets)
    row = lax.broadcasted_iota(jnp.int32, (8, lanes), 0)
    d_tail = jnp.where(row == 0, d_value, 0.0)
    cot = jnp.concatenate([d_logits, d_tail], axis=0).astype(jnp.bfloat16)
    zeros = jnp.zeros((GRAD_ROWS, BLOCK), jnp.float32)
    for side_of in range(2):
        keep_ref[side_of] = zeros
        send_ref[side_of] = zeros
    core = place_ref[0]
    quarter = half // 2
    for side_of in range(2):
        for j in range(quarter):
            rows = slice(j * NUM_HEADS, (j + 1) * NUM_HEADS)
            for ref, who in ((keep_ref, core), (send_ref, 1 - core)):
                part = traj[side_of * half + who * quarter + j]
                out = jnp.dot(cot, part, preferred_element_type=jnp.float32)
                ref[side_of, rows, :] = out[:NUM_HEADS]


def rollout(table, rows_own, rows_other, obs, starts, terms_own, rec_own, parts_a, parts_b):
    steps = starts.shape[1]
    agents = starts.shape[0] // 2
    half = rec_own.shape[1]
    cols, width, lanes = 2 * half, half * BLOCK, steps * agents
    vmem, smem, anywhere = [
        pl.BlockSpec(memory_space=m) for m in (pltpu.VMEM, pltpu.SMEM, pl.ANY)
    ]
    parts = list(parts_a) + list(parts_b)
    return pl.pallas_call(
        rollout_kernel,
        in_specs=[smem] * 3 + [vmem] * 3 + [anywhere] * (1 + len(parts)),
        out_specs=[vmem] * 4,
        out_shape=[
            jax.ShapeDtypeStruct((cols, lanes, BLOCK), jnp.bfloat16),
            jax.ShapeDtypeStruct((agents, width), jnp.bfloat16),
            jax.ShapeDtypeStruct((agents, width), jnp.float32),
            jax.ShapeDtypeStruct((2 * agents, width), jnp.float32),
        ],
        scratch_shapes=[
            pltpu.VMEM((4, half, lanes, BLOCK), jnp.float32),
            pltpu.VMEM((4 * half, 2 * CUT, BLOCK), jnp.bfloat16),
            pltpu.VMEM(rec_own.shape, jnp.bfloat16),
            pltpu.VMEM((cols, agents, BLOCK), jnp.bfloat16),
            pltpu.VMEM((cols, agents, BLOCK), jnp.bfloat16),
            pltpu.VMEM((cols, agents, BLOCK), jnp.float32),
            pltpu.SemaphoreType.DMA((8 * half + 1,)),
        ],
        compiler_params=pltpu.CompilerParams(vmem_limit_bytes=VMEM_LIMIT),
    )(table, rows_own, rows_other, obs, starts, terms_own, rec_own, *parts)


def head_grads(place, traj, head_own, head_other, side, counts):
    vmem = pl.BlockSpec(memory_space=pltpu.VMEM)
    return pl.pallas_call(
        head_kernel,
        in_specs=[pl.BlockSpec(memory_space=pltpu.SMEM)]
        + [vmem] * 4
        + [pl.BlockSpec(memory_space=pl.ANY)],
        out_specs=[vmem] * 2,
        out_shape=[jax.ShapeDtypeStruct((2, GRAD_ROWS, BLOCK), jnp.float32)] * 2,
        scratch_shapes=[
            pltpu.VMEM((counts.shape[0], 8, BLOCK), jnp.float32),
            pltpu.SemaphoreType.DMA,
        ],
        compiler_params=pltpu.CompilerParams(vmem_limit_bytes=SMALL_LIMIT),
    )(place, traj, head_own, head_other, side, counts)


def assemble_kernel(place_ref, grad_ref, mate_ref, out_ref):
    first = place_ref[0] == 0
    grad, mate = grad_ref[...], mate_ref[...]
    quarters = [jnp.where(first, grad, mate), jnp.where(first, mate, grad)]
    per = out_ref.shape[1] // (2 * BLOCK)
    for i in range(2):
        for j in range(per):
            c = i * per + j
            rows = slice(j * NUM_HEADS, (j + 1) * NUM_HEADS)
            out_ref[:, c * BLOCK : (c + 1) * BLOCK] = quarters[i][rows, :]


def assemble(place, grad, mate):
    vmem = pl.BlockSpec(memory_space=pltpu.VMEM)
    per = grad.shape[0] // NUM_HEADS
    return pl.pallas_call(
        assemble_kernel,
        in_specs=[pl.BlockSpec(memory_space=pltpu.SMEM)] + [vmem] * 2,
        out_specs=vmem,
        out_shape=jax.ShapeDtypeStruct((NUM_HEADS, 2 * per * BLOCK), jnp.float32),
    )(place, grad, mate)


def swap(v, axis="blk"):
    return lax.ppermute(v, axis, [(0, 1), (1, 0)])


def ring(v, axis):
    size = lax.axis_size(axis)
    return [v] + [
        lax.ppermute(v, axis, [(i, (i + k) % size) for i in range(size)])
        for k in range(1, size)
    ]


def sum_over(v, axes):
    for axis in axes:
        v = sum(ring(v, axis)[1:], v)
    return v


def shards(
    observations,
    in_weight,
    rec_blocks,
    block_rows,
    episode_start,
    actions,
    rewards,
    mu_logp,
    head_weight,
    learner_of,
):
    blk = lax.axis_index("blk")
    num_agents, num_steps, obs_width = observations.shape
    mine = num_agents // 2
    cols = rec_blocks.shape[1]
    place_y, place_x, place_core = [lax.axis_index(a) for a in ("y", "x", "core")]
    gate, col = place_y, 2 * place_x + place_core
    in_part = lax.dynamic_slice(in_weight, (0, gate, col * BLOCK), (obs_width, 1, BLOCK))
    rec_part = lax.dynamic_slice(
        rec_blocks, (gate, col, 0, 0, 0), (1, 1) + rec_blocks.shape[2:]
    )
    packed = jnp.concatenate(
        [in_part.reshape(-1, BLOCK), rec_part.reshape(-1, BLOCK)], axis=0
    )
    head_own = jnp.pad(head_weight.T, ((0, HEAD_ROWS - head_weight.shape[1]), (0, 0)))
    rows_own = block_rows.reshape(-1)
    packed, rows_other, head_other = lax.optimization_barrier(
        (swap(packed), swap(rows_own), swap(head_own))
    )
    over_x = jnp.concatenate(ring(packed[:CUT], "x"), axis=0)
    over_y = jnp.concatenate(ring(packed[CUT:], "y"), axis=0)

    onehot = learner_of == jnp.arange(BLOCK, dtype=jnp.int32)[None, :]
    counts = jnp.sum(onehot.astype(jnp.float32), axis=0, keepdims=True)
    counts = jnp.broadcast_to(counts, (COUNT_ROWS, BLOCK))

    back = jnp.arange(4, dtype=jnp.int32)
    from_y, from_x = (place_y - back) % 4, (place_x - back) % 4
    from_core = jnp.stack([place_core, 1 - place_core])
    index = (
        8 * from_y[None, :, None] + 2 * from_x[None, None, :] + from_core[:, None, None]
    )
    table = jnp.concatenate(
        [
            index.reshape(-1),
            jnp.swapaxes(index, 1, 2).reshape(-1),
            jnp.stack([cols * blk, mine * blk]),
        ]
    ).astype(jnp.int32)

    starts = episode_start.astype(jnp.float32)
    next_start = jnp.concatenate([starts[:, 1:], jnp.zeros_like(starts[:, :1])], axis=1)
    side = jnp.stack(
        [
            rewards,
            mu_logp,
            actions.astype(jnp.float32),
            next_start,
            jnp.broadcast_to(learner_of.astype(jnp.float32), rewards.shape),
        ]
        + [jnp.zeros_like(rewards)] * 3
    )
    side = lax.dynamic_slice_in_dim(side, blk * mine, mine, 1)
    side = jnp.swapaxes(side, 1, 2).reshape(8, num_steps * mine)
    obs = lax.dynamic_slice_in_dim(observations, blk * mine, mine, 0)
    obs = jnp.swapaxes(obs, 0, 1).reshape(num_steps * mine, obs_width)

    over_x, over_y, obs, side, table, rows_own, rows_other, counts = lax.optimization_barrier(
        (over_x, over_y, obs, side, table, rows_own, rows_other, counts)
    )
    counts = lax.all_gather(counts, ("x", "z", "core"))
    parts_a, parts_b, terms_own = lax.optimization_barrier(
        (ring(over_x, "y"), ring(over_y, "x"), input_terms(obs, in_weight))
    )
    parts_a = parts_a + [swap(p, "core") for p in parts_a]
    parts_b = parts_b + [swap(p, "core") for p in parts_b]

    traj, hidden_own, cell_own, states = rollout(
        table, rows_own, rows_other, obs, episode_start, terms_own, rec_blocks, parts_a, parts_b
    )
    mate = place_core.reshape(1).astype(jnp.int32)
    kept, sent = head_grads(mate, traj, head_own, head_other, side, counts)
    kept = kept + swap(sent, "core")
    grad, states = lax.optimization_barrier((kept[0] + swap(kept[1]), states))
    grad, states = lax.optimization_barrier((sum_over(grad, ("y", "x")), swap(states)))
    grad = sum_over(grad, ("z",))
    grad_mate = swap(grad, "core")
    head_grad = assemble(mate, grad, grad_mate).T

    def place(here, there):
        first = jnp.where(blk == 0, here, there)
        second = jnp.where(blk == 0, there, here)
        return jnp.concatenate([first, second], axis=0)

    cell_last = place(cell_own, states[:mine])
    hidden_last = place(hidden_own, states[mine:].astype(jnp.bfloat16))
    return (head_grad, hidden_last, cell_last)


def solution(mesh):
    fine = Mesh(mesh.devices.reshape(4, 4, 4, 2, 2), ("y", "x", "z", "core", "blk"))
    rows = TORUS
    return jax.shard_map(
        shards,
        mesh=fine,
        in_specs=(
            P(rows, None, None),
            P(None, None, "blk"),
            P(None, "blk", None, None, None),
            P(None, "blk", None),
            P(rows, None),
            P(rows, None),
            P(rows, None),
            P(rows, None),
            P("blk", None),
            P(rows, None),
        ),
        out_specs=(P("blk", None), P(rows, "blk"), P(rows, "blk")),
        check_vma=False,
    )
```

```python
import jax
import jax.numpy as jnp
from jax import lax
from jax.experimental import pallas as pl
from jax.experimental.pallas import tpu as pltpu
from jax.sharding import Mesh, PartitionSpec as P

GAMMA_RATE = 0.99
BLOCK = 128
HEADS = 24
HEAD_ROWS = 32
STEPS = 32
RING_PARTS = 8
ROWS_A = 400
ROWS_B = 384
PAD = 16
NUM_HEADS = 17
GRAD_ROWS = 72
VMEM_LIMIT = 32 * 1024 * 1024
SMALL_LIMIT = 16 * 1024 * 1024
TORUS = ("y", "x", "z", "core")


def sigmoid(x):
    return 0.5 * jnp.tanh(0.5 * x) + 0.5


def input_kernel(obs_ref, weight_ref, out_ref):
    wide = 2 * BLOCK

    def body(i, _):
        for g in range(4):
            w = weight_ref[:, g, pl.ds(pl.multiple_of(i * wide, wide), wide)]
            out = jnp.dot(obs_ref[...], w, preferred_element_type=jnp.float32)
            for j in range(2):
                out_ref[g, 2 * i + j] = out[:, j * BLOCK : (j + 1) * BLOCK]
        return 0

    lax.fori_loop(0, weight_ref.shape[2] // wide, body, 0)


def input_terms(obs, weight):
    vmem = pl.BlockSpec(memory_space=pltpu.VMEM)
    return pl.pallas_call(
        input_kernel,
        in_specs=[vmem] * 2,
        out_specs=vmem,
        out_shape=jax.ShapeDtypeStruct(
            (4, weight.shape[2] // BLOCK, obs.shape[0], BLOCK), jnp.float32
        ),
        compiler_params=pltpu.CompilerParams(vmem_limit_bytes=SMALL_LIMIT),
    )(obs, weight)


def rollout_kernel(
    table_ref, rows_own_ref, rows_other_ref, obs_ref, starts_ref, terms_own_ref, rec_hbm, *refs
):
    parts_a, parts_b = refs[:RING_PARTS], refs[RING_PARTS : 2 * RING_PARTS]
    traj, hidden_own_ref, cell_own_ref, states_ref, counts_ref, head_ref = refs[
        2 * RING_PARTS : 2 * RING_PARTS + 6
    ]
    terms_other, other_a, other_b, rec_own_ref, told, keeps, state_a, state_b, cell, sems = refs[
        2 * RING_PARTS + 6 :
    ]
    steps = starts_ref.shape[1]
    agents = starts_ref.shape[0] // 2
    cols = traj.shape[0]
    half = cols // 2
    lanes = steps * agents
    obs_width = obs_ref.shape[1]
    rec_rows = 4 * BLOCK
    size = 2 * half * 2
    own_at = table_ref[2 * size]
    other_at = half - own_at
    copies = []
    for parts, other_ref in ((parts_a, other_a), (parts_b, other_b)):
        rows = other_ref.shape[1]
        for part in parts:
            for k in range(4):
                n = len(copies)
                copies.append(
                    pltpu.make_async_copy(
                        part.at[pl.ds(k * rows, rows)], other_ref.at[table_ref[n]], sems.at[n]
                    )
                )
    for i, part in enumerate(parts_b):
        copies.append(
            pltpu.make_async_copy(
                part.at[pl.ds(4 * ROWS_B, PAD)], told.at[i], sems.at[len(copies)]
            )
        )
    copies.append(pltpu.make_async_copy(rec_hbm, rec_own_ref, sems.at[len(copies)]))
    for copy in copies:
        copy.start()
    begins = starts_ref[pl.ds(pl.multiple_of(table_ref[2 * size + 1], agents), agents), :]
    begins = begins.astype(jnp.float32)
    for t in range(1, steps):
        keeps[t - 1] = jnp.broadcast_to(1.0 - begins[:, t : t + 1], (agents, BLOCK))
    keeps[steps - 1] = jnp.ones((agents, BLOCK), jnp.float32)
    for copy in copies[:size]:
        copy.wait()

    def in_other(i, _):
        for g in range(4):
            w = jnp.concatenate(
                [other_a[g * half + 2 * i + j, :obs_width, :] for j in range(2)], axis=1
            )
            out = jnp.dot(obs_ref[...], w, preferred_element_type=jnp.float32)
            for j in range(2):
                terms_other[g, 2 * i + j] = out[:, j * BLOCK : (j + 1) * BLOCK]
        return 0

    lax.fori_loop(0, half // 2, in_other, 0)
    for copy in copies[size:]:
        copy.wait()
    for n in range(2 * half):
        piece = other_a[n, obs_width : obs_width + PAD, :]
        head_ref[n % 2 * PAD : n % 2 * PAD + PAD, n // 2 * BLOCK : (n // 2 + 1) * BLOCK] = piece
    counts_ref[...] = sum([told[i].astype(jnp.float32) for i in range(RING_PARTS)])

    state_a[...] = jnp.zeros_like(state_a)
    cell[...] = jnp.zeros_like(cell)

    def step(t, state, state_next):
        base = pl.multiple_of(t * agents, agents)
        keep = keeps[t]
        for c in range(cols):
            own, cc = c < half, c % half
            terms_ref = terms_own_ref if own else terms_other
            rows_ref = rows_own_ref if own else rows_other_ref
            at = (own_at if own else other_at) + cc
            pre = []
            for g in range(4):
                parts = [state[rows_ref[(g * half + cc) * 4 + k]] for k in range(4)]
                lhs = jnp.concatenate(parts, axis=1)
                if own:
                    rhs = rec_own_ref[g, cc].reshape(rec_rows, BLOCK)
                else:
                    n = g * half + cc
                    rhs = jnp.concatenate([other_a[n, obs_width + PAD :, :], other_b[n]], axis=0)
                pre.append(
                    terms_ref[g, cc, pl.ds(base, agents), :]
                    + jnp.dot(lhs, rhs, preferred_element_type=jnp.float32)
                )
            new_cell = sigmoid(pre[1]) * cell[c] + sigmoid(pre[0]) * jnp.tanh(pre[2])
            new_hidden = (sigmoid(pre[3]) * jnp.tanh(new_cell)).astype(jnp.bfloat16)
            traj[c, pl.ds(base, agents), :] = new_hidden
            state_next[at] = (new_hidden * keep).astype(jnp.bfloat16)
            block = slice(cc * BLOCK, (cc + 1) * BLOCK)
            if own:
                cell_own_ref[:, block] = new_cell
            else:
                states_ref[:agents, block] = new_cell
            cell[c] = new_cell * keep

    def two_steps(i, _):
        step(2 * i, state_a, state_b)
        step(2 * i + 1, state_b, state_a)
        return 0

    lax.fori_loop(0, steps // 2, two_steps, 0)
    for c in range(half):
        block = slice(c * BLOCK, (c + 1) * BLOCK)
        hidden_own_ref[:, block] = traj[c, lanes - agents :, :]
        states_ref[agents:, block] = traj[half + c, lanes - agents :, :].astype(jnp.float32)


def head_kernel(
    place_ref, traj, head_own_ref, head_other_ref, side_ref, counts_ref, keep_ref, send_ref
):
    cols, lanes, _ = traj.shape
    half = cols // 2
    agents = lanes // STEPS
    out = jnp.zeros((HEAD_ROWS, lanes), jnp.float32)
    for c in range(cols):
        head_ref, cc = (head_own_ref if c < half else head_other_ref), c % half
        out = out + lax.dot_general(
            head_ref[:, cc * BLOCK : (cc + 1) * BLOCK],
            traj[c],
            (((1,), (1,)), ((), ())),
            preferred_element_type=jnp.float32,
        )
    logits = out[:16]
    value = out[16:17]
    side = side_ref[...]
    rewards, mu_logp, actions, next_start, learner = [side[i : i + 1] for i in range(5)]
    named = lax.broadcasted_iota(jnp.int32, (BLOCK, lanes), 0).astype(jnp.float32) == learner
    count = jnp.dot(
        counts_ref[...].astype(jnp.bfloat16),
        named.astype(jnp.bfloat16),
        preferred_element_type=jnp.float32,
    )[:1]
    weight = 1.0 / (jnp.maximum(count, 1.0) * STEPS)
    top = jnp.max(logits, axis=0, keepdims=True)
    shifted = jnp.exp(logits - top)
    total = jnp.sum(shifted, axis=0, keepdims=True)
    probs = shifted / total
    log_total = jnp.log(total) + top
    which = lax.broadcasted_iota(jnp.int32, logits.shape, 0).astype(jnp.float32)
    picked = (which == actions).astype(jnp.float32)
    logp = jnp.sum(picked * logits, axis=0, keepdims=True) - log_total
    rho = jnp.minimum(1.0, jnp.exp(logp - mu_logp))
    discount = GAMMA_RATE * (1.0 - next_start)
    lane = lax.broadcasted_iota(jnp.int32, value.shape, 1)
    last = lane >= lanes - agents

    def ahead(x, by):
        return pltpu.roll(x, lanes - by, 1)

    value_next = jnp.where(last, value, ahead(value, agents))
    acc = rho * (rewards + discount * value_next - value)
    factor = discount * rho
    by = agents
    while by < lanes:
        out_of = lane >= lanes - by
        acc = acc + factor * jnp.where(out_of, 0.0, ahead(acc, by))
        factor = factor * jnp.where(out_of, 0.0, ahead(factor, by))
        by *= 2
    targets = value + acc
    target_next = jnp.where(last, value, ahead(targets, agents))
    advantage = rho * (rewards + discount * target_next - value)
    d_logits = -(weight * advantage) * (picked - probs)
    d_value = weight * (value - targets)
    row = lax.broadcasted_iota(jnp.int32, (8, lanes), 0)
    d_tail = jnp.where(row == 0, d_value, 0.0)
    cot = jnp.concatenate([d_logits, d_tail], axis=0).astype(jnp.bfloat16)
    zeros = jnp.zeros((GRAD_ROWS, BLOCK), jnp.float32)
    for side_of in range(2):
        keep_ref[side_of] = zeros
        send_ref[side_of] = zeros
    core = place_ref[0]
    quarter = half // 2
    for side_of in range(2):
        for j in range(quarter):
            rows = slice(j * NUM_HEADS, (j + 1) * NUM_HEADS)
            for ref, who in ((keep_ref, core), (send_ref, 1 - core)):
                part = traj[side_of * half + who * quarter + j]
                out = jnp.dot(cot, part, preferred_element_type=jnp.float32)
                ref[side_of, rows, :] = out[:NUM_HEADS]


def rollout(table, rows_own, rows_other, obs, starts, terms_own, rec_own, parts_a, parts_b):
    steps = starts.shape[1]
    agents = starts.shape[0] // 2
    half = rec_own.shape[1]
    cols, width, lanes = 2 * half, half * BLOCK, steps * agents
    vmem, smem, anywhere = [
        pl.BlockSpec(memory_space=m) for m in (pltpu.VMEM, pltpu.SMEM, pl.ANY)
    ]
    parts = list(parts_a) + list(parts_b)
    return pl.pallas_call(
        rollout_kernel,
        in_specs=[smem] * 3 + [vmem] * 3 + [anywhere] * (1 + len(parts)),
        out_specs=[vmem] * 6,
        out_shape=[
            jax.ShapeDtypeStruct((cols, lanes, BLOCK), jnp.bfloat16),
            jax.ShapeDtypeStruct((agents, width), jnp.bfloat16),
            jax.ShapeDtypeStruct((agents, width), jnp.float32),
            jax.ShapeDtypeStruct((2 * agents, width), jnp.float32),
            jax.ShapeDtypeStruct((PAD, BLOCK), jnp.float32),
            jax.ShapeDtypeStruct((HEAD_ROWS, width), jnp.bfloat16),
        ],
        scratch_shapes=[
            pltpu.VMEM((4, half, lanes, BLOCK), jnp.float32),
            pltpu.VMEM((4 * half, ROWS_A, BLOCK), jnp.bfloat16),
            pltpu.VMEM((4 * half, ROWS_B, BLOCK), jnp.bfloat16),
            pltpu.VMEM(rec_own.shape, jnp.bfloat16),
            pltpu.VMEM((RING_PARTS, PAD, BLOCK), jnp.bfloat16),
            pltpu.VMEM((steps, agents, BLOCK), jnp.float32),
            pltpu.VMEM((cols, agents, BLOCK), jnp.bfloat16),
            pltpu.VMEM((cols, agents, BLOCK), jnp.bfloat16),
            pltpu.VMEM((cols, agents, BLOCK), jnp.float32),
            pltpu.SemaphoreType.DMA((8 * half + RING_PARTS + 1,)),
        ],
        compiler_params=pltpu.CompilerParams(vmem_limit_bytes=VMEM_LIMIT),
    )(table, rows_own, rows_other, obs, starts, terms_own, rec_own, *parts)


def head_grads(place, traj, head_own, head_other, side, counts):
    vmem = pl.BlockSpec(memory_space=pltpu.VMEM)
    return pl.pallas_call(
        head_kernel,
        in_specs=[pl.BlockSpec(memory_space=pltpu.SMEM)] + [vmem] * 5,
        out_specs=[vmem] * 2,
        out_shape=[jax.ShapeDtypeStruct((2, GRAD_ROWS, BLOCK), jnp.float32)] * 2,
        compiler_params=pltpu.CompilerParams(vmem_limit_bytes=SMALL_LIMIT),
    )(place, traj, head_own, head_other, side, counts)


def assemble_kernel(place_ref, grad_ref, mate_ref, out_ref):
    first = place_ref[0] == 0
    grad, mate = grad_ref[...], mate_ref[...]
    quarters = [jnp.where(first, grad, mate), jnp.where(first, mate, grad)]
    per = out_ref.shape[1] // (2 * BLOCK)
    for i in range(2):
        for j in range(per):
            c = i * per + j
            rows = slice(j * NUM_HEADS, (j + 1) * NUM_HEADS)
            out_ref[:, c * BLOCK : (c + 1) * BLOCK] = quarters[i][rows, :]


def assemble(place, grad, mate):
    vmem = pl.BlockSpec(memory_space=pltpu.VMEM)
    per = grad.shape[0] // NUM_HEADS
    return pl.pallas_call(
        assemble_kernel,
        in_specs=[pl.BlockSpec(memory_space=pltpu.SMEM)] + [vmem] * 2,
        out_specs=vmem,
        out_shape=jax.ShapeDtypeStruct((NUM_HEADS, 2 * per * BLOCK), jnp.float32),
    )(place, grad, mate)


def join_kernel(*refs):
    at = 0
    for ref in refs[:-1]:
        rows = ref.shape[0]
        refs[-1][at : at + rows, :] = ref[...]
        at += rows


def join(parts):
    vmem = pl.BlockSpec(memory_space=pltpu.VMEM)
    rows = sum([p.shape[0] for p in parts])
    return pl.pallas_call(
        join_kernel,
        in_specs=[vmem] * len(parts),
        out_specs=vmem,
        out_shape=jax.ShapeDtypeStruct((rows, BLOCK), parts[0].dtype),
    )(*parts)


def swap(v, axis="blk"):
    return lax.ppermute(v, axis, [(0, 1), (1, 0)])


def ring(v, axis):
    size = lax.axis_size(axis)
    return [v] + [
        lax.ppermute(v, axis, [(i, (i + k) % size) for i in range(size)])
        for k in range(1, size)
    ]


def sum_over(v, axes):
    for axis in axes:
        v = sum(ring(v, axis)[1:], v)
    return v


def shards(
    observations,
    in_weight,
    rec_blocks,
    block_rows,
    episode_start,
    actions,
    rewards,
    mu_logp,
    head_weight,
    learner_of,
):
    blk = lax.axis_index("blk")
    num_agents, num_steps, obs_width = observations.shape
    mine = num_agents // 2
    cols = rec_blocks.shape[1]
    place_y, place_x, place_core = [lax.axis_index(a) for a in ("y", "x", "core")]
    gate, col = place_y, 2 * place_x + place_core
    in_part = lax.dynamic_slice(in_weight, (0, gate, col * BLOCK), (obs_width, 1, BLOCK))
    rec_part = lax.dynamic_slice(
        rec_blocks, (gate, col, 0, 0, 0), (1, 1) + rec_blocks.shape[2:]
    )
    head_own = jnp.pad(head_weight.T, ((0, HEAD_ROWS - head_weight.shape[1]), (0, 0)))
    piece = (cols * gate + col) % (2 * cols)
    head_part = lax.dynamic_slice(
        head_own, (piece % 2 * PAD, piece // 2 * BLOCK), (PAD, BLOCK)
    )
    packed = join([in_part.reshape(-1, BLOCK), head_part, rec_part.reshape(-1, BLOCK)])
    rows_own = block_rows.reshape(-1)
    packed, rows_other, learner = lax.optimization_barrier(
        (swap(packed), swap(rows_own), learner_of)
    )
    onehot = learner == jnp.arange(BLOCK, dtype=jnp.int32)[None, :]
    counts = jnp.sum(onehot.astype(jnp.bfloat16), axis=0, keepdims=True)
    counts = sum_over(jnp.broadcast_to(counts, (PAD, BLOCK)), ("z",))
    over_x = join(ring(packed[:ROWS_A], "x"))
    over_y = join(ring(packed[ROWS_A:], "y") + [counts])

    back = jnp.arange(4, dtype=jnp.int32)
    from_y, from_x = (place_y - back) % 4, (place_x - back) % 4
    from_core = jnp.stack([place_core, 1 - place_core])
    index = (
        8 * from_y[None, :, None] + 2 * from_x[None, None, :] + from_core[:, None, None]
    )
    table = jnp.concatenate(
        [
            index.reshape(-1),
            jnp.swapaxes(index, 1, 2).reshape(-1),
            jnp.stack([cols * blk, mine * blk]),
        ]
    ).astype(jnp.int32)

    starts = episode_start.astype(jnp.float32)
    next_start = jnp.concatenate([starts[:, 1:], jnp.zeros_like(starts[:, :1])], axis=1)
    side = jnp.stack(
        [
            rewards,
            mu_logp,
            actions.astype(jnp.float32),
            next_start,
            jnp.broadcast_to(learner_of.astype(jnp.float32), rewards.shape),
        ]
        + [jnp.zeros_like(rewards)] * 3
    )
    side = lax.dynamic_slice_in_dim(side, blk * mine, mine, 1)
    side = jnp.swapaxes(side, 1, 2).reshape(8, num_steps * mine)
    obs = lax.dynamic_slice_in_dim(observations, blk * mine, mine, 0)
    obs = jnp.swapaxes(obs, 0, 1).reshape(num_steps * mine, obs_width)

    over_x, over_y, obs, side, table, rows_own, rows_other = lax.optimization_barrier(
        (over_x, over_y, obs, side, table, rows_own, rows_other)
    )
    parts_a, parts_b, terms_own = lax.optimization_barrier(
        (ring(over_x, "y"), ring(over_y, "x"), input_terms(obs, in_weight))
    )
    parts_a = parts_a + [swap(p, "core") for p in parts_a]
    parts_b = parts_b + [swap(p, "core") for p in parts_b]

    traj, hidden_own, cell_own, states, counts, head_other = rollout(
        table, rows_own, rows_other, obs, episode_start, terms_own, rec_blocks, parts_a, parts_b
    )
    mate = place_core.reshape(1).astype(jnp.int32)
    kept, sent = head_grads(mate, traj, head_own, head_other, side, counts)
    kept = kept + swap(sent, "core")
    states = swap(states)
    grad = sum_over(kept[0] + swap(kept[1]), ("y", "x", "z"))
    grad_mate = swap(grad, "core")
    head_grad = assemble(mate, grad, grad_mate).T

    def place(here, there):
        first = jnp.where(blk == 0, here, there)
        second = jnp.where(blk == 0, there, here)
        return jnp.concatenate([first, second], axis=0)

    cell_last = place(cell_own, states[:mine])
    hidden_last = place(hidden_own, states[mine:].astype(jnp.bfloat16))
    return (head_grad, hidden_last, cell_last)


def solution(mesh):
    fine = Mesh(mesh.devices.reshape(4, 4, 4, 2, 2), ("y", "x", "z", "core", "blk"))
    rows = TORUS
    return jax.shard_map(
        shards,
        mesh=fine,
        in_specs=(
            P(rows, None, None),
            P(None, None, "blk"),
            P(None, "blk", None, None, None),
            P(None, "blk", None),
            P(rows, None),
            P(rows, None),
            P(rows, None),
            P(rows, None),
            P("blk", None),
            P(rows, None),
        ),
        out_specs=(P("blk", None), P(rows, "blk"), P(rows, "blk")),
        check_vma=False,
    )
```

```python
import jax
import jax.numpy as jnp
from jax import lax
from jax.experimental import pallas as pl
from jax.experimental.pallas import tpu as pltpu
from jax.sharding import Mesh, PartitionSpec as P

GAMMA_RATE = 0.99
BLOCK = 128
HEADS = 24
HEAD_ROWS = 32
STEPS = 32
RING_PARTS = 8
ROWS_A = 400
ROWS_B = 384
PAD = 16
NUM_HEADS = 17
GRAD_ROWS = 72
VMEM_LIMIT = 32 * 1024 * 1024
SMALL_LIMIT = 16 * 1024 * 1024
TORUS = ("y", "x", "z", "core")


def sigmoid(x):
    return 0.5 * jnp.tanh(0.5 * x) + 0.5


def input_kernel(obs_ref, weight_ref, out_ref):
    wide = 2 * BLOCK

    def body(i, _):
        for g in range(4):
            w = weight_ref[:, g, pl.ds(pl.multiple_of(i * wide, wide), wide)]
            out = jnp.dot(obs_ref[...], w, preferred_element_type=jnp.float32)
            for j in range(2):
                out_ref[g, 2 * i + j] = out[:, j * BLOCK : (j + 1) * BLOCK]
        return 0

    lax.fori_loop(0, weight_ref.shape[2] // wide, body, 0)


def input_terms(obs, weight):
    vmem = pl.BlockSpec(memory_space=pltpu.VMEM)
    return pl.pallas_call(
        input_kernel,
        in_specs=[vmem] * 2,
        out_specs=vmem,
        out_shape=jax.ShapeDtypeStruct(
            (4, weight.shape[2] // BLOCK, obs.shape[0], BLOCK), jnp.float32
        ),
        compiler_params=pltpu.CompilerParams(vmem_limit_bytes=SMALL_LIMIT),
    )(obs, weight)


def rollout_kernel(
    table_ref, rows_own_ref, rows_other_ref, obs_ref, starts_ref, terms_own_ref, rec_own_ref, *refs
):
    parts_a, parts_b = refs[:RING_PARTS], refs[RING_PARTS : 2 * RING_PARTS]
    traj, hidden_own_ref, cell_own_ref, states_ref, counts_ref, head_ref = refs[
        2 * RING_PARTS : 2 * RING_PARTS + 6
    ]
    terms_other, other_a, other_b, keeps, state_a, state_b, cell = refs[
        2 * RING_PARTS + 6 :
    ]
    steps = starts_ref.shape[1]
    agents = starts_ref.shape[0] // 2
    cols = traj.shape[0]
    half = cols // 2
    lanes = steps * agents
    obs_width = obs_ref.shape[1]
    rec_rows = 4 * BLOCK
    size = 2 * half * 2
    own_at = table_ref[2 * size]
    other_at = half - own_at
    n = 0
    for parts, other_ref in ((parts_a, other_a), (parts_b, other_b)):
        rows = other_ref.shape[1]
        for part in parts:
            for k in range(4):
                other_ref[table_ref[n]] = part[k * rows : (k + 1) * rows, :]
                n += 1
    begins = starts_ref[pl.ds(pl.multiple_of(table_ref[2 * size + 1], agents), agents), :]
    begins = begins.astype(jnp.float32)
    for t in range(1, steps):
        keeps[t - 1] = jnp.broadcast_to(1.0 - begins[:, t : t + 1], (agents, BLOCK))
    keeps[steps - 1] = jnp.ones((agents, BLOCK), jnp.float32)

    def in_other(i, _):
        for g in range(4):
            w = jnp.concatenate(
                [other_a[g * half + 2 * i + j, :obs_width, :] for j in range(2)], axis=1
            )
            out = jnp.dot(obs_ref[...], w, preferred_element_type=jnp.float32)
            for j in range(2):
                terms_other[g, 2 * i + j] = out[:, j * BLOCK : (j + 1) * BLOCK]
        return 0

    lax.fori_loop(0, half // 2, in_other, 0)
    for n in range(2 * half):
        piece = other_a[n, obs_width : obs_width + PAD, :]
        head_ref[n % 2 * PAD : n % 2 * PAD + PAD, n // 2 * BLOCK : (n // 2 + 1) * BLOCK] = piece
    told = [part[4 * ROWS_B :, :].astype(jnp.float32) for part in parts_b]
    counts_ref[...] = sum(told[1:], told[0])

    state_a[...] = jnp.zeros_like(state_a)
    cell[...] = jnp.zeros_like(cell)

    def step(t, state, state_next):
        base = pl.multiple_of(t * agents, agents)
        keep = keeps[t]
        for c in range(cols):
            own, cc = c < half, c % half
            terms_ref = terms_own_ref if own else terms_other
            rows_ref = rows_own_ref if own else rows_other_ref
            at = (own_at if own else other_at) + cc
            pre = []
            for g in range(4):
                parts = [state[rows_ref[(g * half + cc) * 4 + k]] for k in range(4)]
                lhs = jnp.concatenate(parts, axis=1)
                if own:
                    rhs = rec_own_ref[g, cc].reshape(rec_rows, BLOCK)
                else:
                    n = g * half + cc
                    rhs = jnp.concatenate([other_a[n, obs_width + PAD :, :], other_b[n]], axis=0)
                pre.append(
                    terms_ref[g, cc, pl.ds(base, agents), :]
                    + jnp.dot(lhs, rhs, preferred_element_type=jnp.float32)
                )
            new_cell = sigmoid(pre[1]) * cell[c] + sigmoid(pre[0]) * jnp.tanh(pre[2])
            new_hidden = (sigmoid(pre[3]) * jnp.tanh(new_cell)).astype(jnp.bfloat16)
            traj[c, pl.ds(base, agents), :] = new_hidden
            state_next[at] = (new_hidden * keep).astype(jnp.bfloat16)
            block = slice(cc * BLOCK, (cc + 1) * BLOCK)
            if own:
                cell_own_ref[:, block] = new_cell
            else:
                states_ref[:agents, block] = new_cell
            cell[c] = new_cell * keep

    def two_steps(i, _):
        step(2 * i, state_a, state_b)
        step(2 * i + 1, state_b, state_a)
        return 0

    lax.fori_loop(0, steps // 2, two_steps, 0)
    for c in range(half):
        block = slice(c * BLOCK, (c + 1) * BLOCK)
        hidden_own_ref[:, block] = traj[c, lanes - agents :, :]
        states_ref[agents:, block] = traj[half + c, lanes - agents :, :].astype(jnp.float32)


def head_kernel(
    place_ref, traj, head_own_ref, head_other_ref, side_ref, counts_ref, keep_ref, send_ref
):
    cols, lanes, _ = traj.shape
    half = cols // 2
    agents = lanes // STEPS
    out = jnp.zeros((HEAD_ROWS, lanes), jnp.float32)
    for c in range(cols):
        head_ref, cc = (head_own_ref if c < half else head_other_ref), c % half
        out = out + lax.dot_general(
            head_ref[:, cc * BLOCK : (cc + 1) * BLOCK],
            traj[c],
            (((1,), (1,)), ((), ())),
            preferred_element_type=jnp.float32,
        )
    logits = out[:16]
    value = out[16:17]
    side = side_ref[...]
    rewards, mu_logp, actions, next_start, learner = [side[i : i + 1] for i in range(5)]
    named = lax.broadcasted_iota(jnp.int32, (BLOCK, lanes), 0).astype(jnp.float32) == learner
    count = jnp.dot(
        counts_ref[...].astype(jnp.bfloat16),
        named.astype(jnp.bfloat16),
        preferred_element_type=jnp.float32,
    )[:1]
    weight = 1.0 / (jnp.maximum(count, 1.0) * STEPS)
    top = jnp.max(logits, axis=0, keepdims=True)
    shifted = jnp.exp(logits - top)
    total = jnp.sum(shifted, axis=0, keepdims=True)
    probs = shifted / total
    log_total = jnp.log(total) + top
    which = lax.broadcasted_iota(jnp.int32, logits.shape, 0).astype(jnp.float32)
    picked = (which == actions).astype(jnp.float32)
    logp = jnp.sum(picked * logits, axis=0, keepdims=True) - log_total
    rho = jnp.minimum(1.0, jnp.exp(logp - mu_logp))
    discount = GAMMA_RATE * (1.0 - next_start)
    lane = lax.broadcasted_iota(jnp.int32, value.shape, 1)
    last = lane >= lanes - agents

    def ahead(x, by):
        return pltpu.roll(x, lanes - by, 1)

    value_next = jnp.where(last, value, ahead(value, agents))
    acc = rho * (rewards + discount * value_next - value)
    factor = discount * rho
    by = agents
    while by < lanes:
        out_of = lane >= lanes - by
        acc = acc + factor * jnp.where(out_of, 0.0, ahead(acc, by))
        factor = factor * jnp.where(out_of, 0.0, ahead(factor, by))
        by *= 2
    targets = value + acc
    target_next = jnp.where(last, value, ahead(targets, agents))
    advantage = rho * (rewards + discount * target_next - value)
    d_logits = -(weight * advantage) * (picked - probs)
    d_value = weight * (value - targets)
    row = lax.broadcasted_iota(jnp.int32, (8, lanes), 0)
    d_tail = jnp.where(row == 0, d_value, 0.0)
    cot = jnp.concatenate([d_logits, d_tail], axis=0).astype(jnp.bfloat16)
    zeros = jnp.zeros((GRAD_ROWS, BLOCK), jnp.float32)
    for side_of in range(2):
        keep_ref[side_of] = zeros
        send_ref[side_of] = zeros
    core = place_ref[0]
    quarter = half // 2
    for side_of in range(2):
        for j in range(quarter):
            rows = slice(j * NUM_HEADS, (j + 1) * NUM_HEADS)
            for ref, who in ((keep_ref, core), (send_ref, 1 - core)):
                part = traj[side_of * half + who * quarter + j]
                out = jnp.dot(cot, part, preferred_element_type=jnp.float32)
                ref[side_of, rows, :] = out[:NUM_HEADS]


def rollout(table, rows_own, rows_other, obs, starts, terms_own, rec_own, parts_a, parts_b):
    steps = starts.shape[1]
    agents = starts.shape[0] // 2
    half = rec_own.shape[1]
    cols, width, lanes = 2 * half, half * BLOCK, steps * agents
    vmem, smem = [pl.BlockSpec(memory_space=m) for m in (pltpu.VMEM, pltpu.SMEM)]
    parts = list(parts_a) + list(parts_b)
    return pl.pallas_call(
        rollout_kernel,
        in_specs=[smem] * 3 + [vmem] * (4 + len(parts)),
        out_specs=[vmem] * 6,
        out_shape=[
            jax.ShapeDtypeStruct((cols, lanes, BLOCK), jnp.bfloat16),
            jax.ShapeDtypeStruct((agents, width), jnp.bfloat16),
            jax.ShapeDtypeStruct((agents, width), jnp.float32),
            jax.ShapeDtypeStruct((2 * agents, width), jnp.float32),
            jax.ShapeDtypeStruct((PAD, BLOCK), jnp.float32),
            jax.ShapeDtypeStruct((HEAD_ROWS, width), jnp.bfloat16),
        ],
        scratch_shapes=[
            pltpu.VMEM((4, half, lanes, BLOCK), jnp.float32),
            pltpu.VMEM((4 * half, ROWS_A, BLOCK), jnp.bfloat16),
            pltpu.VMEM((4 * half, ROWS_B, BLOCK), jnp.bfloat16),
            pltpu.VMEM((steps, agents, BLOCK), jnp.float32),
            pltpu.VMEM((cols, agents, BLOCK), jnp.bfloat16),
            pltpu.VMEM((cols, agents, BLOCK), jnp.bfloat16),
            pltpu.VMEM((cols, agents, BLOCK), jnp.float32),
        ],
        compiler_params=pltpu.CompilerParams(vmem_limit_bytes=VMEM_LIMIT),
    )(table, rows_own, rows_other, obs, starts, terms_own, rec_own, *parts)


def head_grads(place, traj, head_own, head_other, side, counts):
    vmem = pl.BlockSpec(memory_space=pltpu.VMEM)
    return pl.pallas_call(
        head_kernel,
        in_specs=[pl.BlockSpec(memory_space=pltpu.SMEM)] + [vmem] * 5,
        out_specs=[vmem] * 2,
        out_shape=[jax.ShapeDtypeStruct((2, GRAD_ROWS, BLOCK), jnp.float32)] * 2,
        compiler_params=pltpu.CompilerParams(vmem_limit_bytes=SMALL_LIMIT),
    )(place, traj, head_own, head_other, side, counts)


def assemble_kernel(place_ref, grad_ref, mate_ref, out_ref):
    first = place_ref[0] == 0
    grad, mate = grad_ref[...], mate_ref[...]
    quarters = [jnp.where(first, grad, mate), jnp.where(first, mate, grad)]
    per = out_ref.shape[1] // (2 * BLOCK)
    for i in range(2):
        for j in range(per):
            c = i * per + j
            rows = slice(j * NUM_HEADS, (j + 1) * NUM_HEADS)
            out_ref[:, c * BLOCK : (c + 1) * BLOCK] = quarters[i][rows, :]


def assemble(place, grad, mate):
    vmem = pl.BlockSpec(memory_space=pltpu.VMEM)
    per = grad.shape[0] // NUM_HEADS
    return pl.pallas_call(
        assemble_kernel,
        in_specs=[pl.BlockSpec(memory_space=pltpu.SMEM)] + [vmem] * 2,
        out_specs=vmem,
        out_shape=jax.ShapeDtypeStruct((NUM_HEADS, 2 * per * BLOCK), jnp.float32),
    )(place, grad, mate)


def join_kernel(*refs):
    at = 0
    for ref in refs[:-1]:
        rows = ref.shape[0]
        refs[-1][at : at + rows, :] = ref[...]
        at += rows


def join(parts):
    vmem = pl.BlockSpec(memory_space=pltpu.VMEM)
    rows = sum([p.shape[0] for p in parts])
    return pl.pallas_call(
        join_kernel,
        in_specs=[vmem] * len(parts),
        out_specs=vmem,
        out_shape=jax.ShapeDtypeStruct((rows, BLOCK), parts[0].dtype),
    )(*parts)


def swap(v, axis="blk"):
    return lax.ppermute(v, axis, [(0, 1), (1, 0)])


def ring(v, axis):
    size = lax.axis_size(axis)
    return [v] + [
        lax.ppermute(v, axis, [(i, (i + k) % size) for i in range(size)])
        for k in range(1, size)
    ]


def sum_over(v, axes):
    for axis in axes:
        v = sum(ring(v, axis)[1:], v)
    return v


def shards(
    observations,
    in_weight,
    rec_blocks,
    block_rows,
    episode_start,
    actions,
    rewards,
    mu_logp,
    head_weight,
    learner_of,
):
    blk = lax.axis_index("blk")
    num_agents, num_steps, obs_width = observations.shape
    mine = num_agents // 2
    cols = rec_blocks.shape[1]
    place_y, place_x, place_core = [lax.axis_index(a) for a in ("y", "x", "core")]
    gate, col = place_y, 2 * place_x + place_core
    in_part = lax.dynamic_slice(in_weight, (0, gate, col * BLOCK), (obs_width, 1, BLOCK))
    rec_part = lax.dynamic_slice(
        rec_blocks, (gate, col, 0, 0, 0), (1, 1) + rec_blocks.shape[2:]
    )
    head_own = jnp.pad(head_weight.T, ((0, HEAD_ROWS - head_weight.shape[1]), (0, 0)))
    piece = (cols * gate + col) % (2 * cols)
    head_part = lax.dynamic_slice(
        head_own, (piece % 2 * PAD, piece // 2 * BLOCK), (PAD, BLOCK)
    )
    packed = join([in_part.reshape(-1, BLOCK), head_part, rec_part.reshape(-1, BLOCK)])
    rows_own = block_rows.reshape(-1)
    packed, rows_other, learner = lax.optimization_barrier(
        (swap(packed), swap(rows_own), learner_of)
    )
    onehot = learner == jnp.arange(BLOCK, dtype=jnp.int32)[None, :]
    counts = jnp.sum(onehot.astype(jnp.bfloat16), axis=0, keepdims=True)
    counts = sum_over(jnp.broadcast_to(counts, (PAD, BLOCK)), ("z",))
    over_x = jnp.concatenate(ring(packed[:ROWS_A], "x"), axis=0)
    over_y = join(ring(packed[ROWS_A:], "y") + [counts])

    back = jnp.arange(4, dtype=jnp.int32)
    from_y, from_x = (place_y - back) % 4, (place_x - back) % 4
    from_core = jnp.stack([place_core, 1 - place_core])
    index = (
        8 * from_y[None, :, None] + 2 * from_x[None, None, :] + from_core[:, None, None]
    )
    table = jnp.concatenate(
        [
            index.reshape(-1),
            jnp.swapaxes(index, 1, 2).reshape(-1),
            jnp.stack([cols * blk, mine * blk]),
        ]
    ).astype(jnp.int32)

    starts = episode_start.astype(jnp.float32)
    next_start = jnp.concatenate([starts[:, 1:], jnp.zeros_like(starts[:, :1])], axis=1)
    side = jnp.stack(
        [
            rewards,
            mu_logp,
            actions.astype(jnp.float32),
            next_start,
            jnp.broadcast_to(learner_of.astype(jnp.float32), rewards.shape),
        ]
        + [jnp.zeros_like(rewards)] * 3
    )
    side = lax.dynamic_slice_in_dim(side, blk * mine, mine, 1)
    side = jnp.swapaxes(side, 1, 2).reshape(8, num_steps * mine)
    obs = lax.dynamic_slice_in_dim(observations, blk * mine, mine, 0)
    obs = jnp.swapaxes(obs, 0, 1).reshape(num_steps * mine, obs_width)

    over_x, over_y, obs, side, table, rows_own, rows_other = lax.optimization_barrier(
        (over_x, over_y, obs, side, table, rows_own, rows_other)
    )
    parts_a, parts_b, terms_own = lax.optimization_barrier(
        (ring(over_x, "y"), ring(over_y, "x"), input_terms(obs, in_weight))
    )
    parts_a = parts_a + [swap(p, "core") for p in parts_a]
    parts_b = parts_b + [swap(p, "core") for p in parts_b]

    traj, hidden_own, cell_own, states, counts, head_other = rollout(
        table, rows_own, rows_other, obs, episode_start, terms_own, rec_blocks, parts_a, parts_b
    )
    mate = place_core.reshape(1).astype(jnp.int32)
    kept, sent = head_grads(mate, traj, head_own, head_other, side, counts)
    kept = kept + swap(sent, "core")
    states = swap(states)
    grad = sum_over(kept[0] + swap(kept[1]), ("y", "x", "z"))
    grad_mate = swap(grad, "core")
    head_grad = assemble(mate, grad, grad_mate).T

    def place(here, there):
        first = jnp.where(blk == 0, here, there)
        second = jnp.where(blk == 0, there, here)
        return jnp.concatenate([first, second], axis=0)

    cell_last = place(cell_own, states[:mine])
    hidden_last = place(hidden_own, states[mine:].astype(jnp.bfloat16))
    return (head_grad, hidden_last, cell_last)


def solution(mesh):
    fine = Mesh(mesh.devices.reshape(4, 4, 4, 2, 2), ("y", "x", "z", "core", "blk"))
    rows = TORUS
    return jax.shard_map(
        shards,
        mesh=fine,
        in_specs=(
            P(rows, None, None),
            P(None, None, "blk"),
            P(None, "blk", None, None, None),
            P(None, "blk", None),
            P(rows, None),
            P(rows, None),
            P(rows, None),
            P(rows, None),
            P("blk", None),
            P(rows, None),
        ),
        out_specs=(P("blk", None), P(rows, "blk"), P(rows, "blk")),
        check_vma=False,
    )
```

```python
import jax
import jax.numpy as jnp
from jax import lax
from jax.experimental import pallas as pl
from jax.experimental.pallas import tpu as pltpu
from jax.sharding import Mesh, PartitionSpec as P

GAMMA_RATE = 0.99
BLOCK = 128
HEADS = 24
HEAD_ROWS = 32
STEPS = 32
RING_PARTS = 8
ROWS_A = 400
ROWS_B = 384
PAD = 16
NUM_HEADS = 17
GRAD_ROWS = 72
VMEM_LIMIT = 32 * 1024 * 1024
SMALL_LIMIT = 16 * 1024 * 1024
TORUS = ("y", "x", "z", "core")


def sigmoid(x):
    return 0.5 * jnp.tanh(0.5 * x) + 0.5


def input_kernel(obs_ref, weight_ref, out_ref):
    wide = 2 * BLOCK

    def body(i, _):
        for g in range(4):
            w = weight_ref[:, g, pl.ds(pl.multiple_of(i * wide, wide), wide)]
            out = jnp.dot(obs_ref[...], w, preferred_element_type=jnp.float32)
            for j in range(2):
                out_ref[g, 2 * i + j] = out[:, j * BLOCK : (j + 1) * BLOCK]
        return 0

    lax.fori_loop(0, weight_ref.shape[2] // wide, body, 0)


def input_terms(obs, weight):
    vmem = pl.BlockSpec(memory_space=pltpu.VMEM)
    return pl.pallas_call(
        input_kernel,
        in_specs=[vmem] * 2,
        out_specs=vmem,
        out_shape=jax.ShapeDtypeStruct(
            (4, weight.shape[2] // BLOCK, obs.shape[0], BLOCK), jnp.float32
        ),
        compiler_params=pltpu.CompilerParams(vmem_limit_bytes=SMALL_LIMIT),
    )(obs, weight)


def rollout_kernel(
    table_ref, rows_own_ref, rows_other_ref, obs_ref, starts_ref, terms_own_ref, rec_own_ref, *refs
):
    parts_a, parts_b = refs[:RING_PARTS], refs[RING_PARTS : 2 * RING_PARTS]
    traj, hidden_own_ref, cell_own_ref, states_ref, counts_ref, head_ref = refs[
        2 * RING_PARTS : 2 * RING_PARTS + 6
    ]
    terms_other, other_a, other_b, keeps, state_a, state_b, cell = refs[
        2 * RING_PARTS + 6 :
    ]
    steps = starts_ref.shape[1]
    agents = starts_ref.shape[0] // 2
    cols = traj.shape[0]
    half = cols // 2
    lanes = steps * agents
    obs_width = obs_ref.shape[1]
    rec_rows = 4 * BLOCK
    size = 2 * half * 2
    own_at = table_ref[2 * size]
    other_at = half - own_at
    n = 0
    for parts, other_ref in ((parts_a, other_a), (parts_b, other_b)):
        rows = other_ref.shape[1]
        for part in parts:
            for k in range(4):
                other_ref[table_ref[n]] = part[k * rows : (k + 1) * rows, :]
                n += 1
    begins = starts_ref[pl.ds(pl.multiple_of(table_ref[2 * size + 1], agents), agents), :]
    begins = begins.astype(jnp.float32)
    for t in range(1, steps):
        keeps[t - 1] = jnp.broadcast_to(1.0 - begins[:, t : t + 1], (agents, BLOCK))
    keeps[steps - 1] = jnp.ones((agents, BLOCK), jnp.float32)

    def in_other(i, _):
        for g in range(4):
            w = jnp.concatenate(
                [other_a[g * half + 2 * i + j, :obs_width, :] for j in range(2)], axis=1
            )
            out = jnp.dot(obs_ref[...], w, preferred_element_type=jnp.float32)
            for j in range(2):
                terms_other[g, 2 * i + j] = out[:, j * BLOCK : (j + 1) * BLOCK]
        return 0

    lax.fori_loop(0, half // 2, in_other, 0)
    for n in range(2 * half):
        piece = other_a[n, obs_width : obs_width + PAD, :]
        head_ref[n % 2 * PAD : n % 2 * PAD + PAD, n // 2 * BLOCK : (n // 2 + 1) * BLOCK] = piece
    told = [part[4 * ROWS_B :, :].astype(jnp.float32) for part in parts_b]
    counts_ref[...] = sum(told[1:], told[0])

    state_a[...] = jnp.zeros_like(state_a)
    cell[...] = jnp.zeros_like(cell)

    def step(t, state, state_next):
        base = pl.multiple_of(t * agents, agents)
        keep = keeps[t]
        for c in range(cols):
            own, cc = c < half, c % half
            terms_ref = terms_own_ref if own else terms_other
            rows_ref = rows_own_ref if own else rows_other_ref
            at = (own_at if own else other_at) + cc
            pre = []
            for g in range(4):
                parts = [state[rows_ref[(g * half + cc) * 4 + k]] for k in range(4)]
                lhs = jnp.concatenate(parts, axis=1)
                if own:
                    rhs = rec_own_ref[g, cc].reshape(rec_rows, BLOCK)
                else:
                    n = g * half + cc
                    rhs = jnp.concatenate([other_a[n, obs_width + PAD :, :], other_b[n]], axis=0)
                pre.append(
                    terms_ref[g, cc, pl.ds(base, agents), :]
                    + jnp.dot(lhs, rhs, preferred_element_type=jnp.float32)
                )
            new_cell = sigmoid(pre[1]) * cell[c] + sigmoid(pre[0]) * jnp.tanh(pre[2])
            new_hidden = (sigmoid(pre[3]) * jnp.tanh(new_cell)).astype(jnp.bfloat16)
            traj[c, pl.ds(base, agents), :] = new_hidden
            state_next[at] = (new_hidden * keep).astype(jnp.bfloat16)
            block = slice(cc * BLOCK, (cc + 1) * BLOCK)
            if own:
                cell_own_ref[:, block] = new_cell
            else:
                states_ref[:agents, block] = new_cell.astype(jnp.bfloat16)
            cell[c] = new_cell * keep

    def two_steps(i, _):
        step(2 * i, state_a, state_b)
        step(2 * i + 1, state_b, state_a)
        return 0

    lax.fori_loop(0, steps // 2, two_steps, 0)
    for c in range(half):
        block = slice(c * BLOCK, (c + 1) * BLOCK)
        hidden_own_ref[:, block] = traj[c, lanes - agents :, :]
        states_ref[agents:, block] = traj[half + c, lanes - agents :, :]


def head_kernel(
    place_ref, traj, head_own_ref, head_other_ref, side_ref, counts_ref, keep_ref, send_ref
):
    cols, lanes, _ = traj.shape
    half = cols // 2
    agents = lanes // STEPS
    out = jnp.zeros((HEAD_ROWS, lanes), jnp.float32)
    for c in range(cols):
        head_ref, cc = (head_own_ref if c < half else head_other_ref), c % half
        out = out + lax.dot_general(
            head_ref[:, cc * BLOCK : (cc + 1) * BLOCK],
            traj[c],
            (((1,), (1,)), ((), ())),
            preferred_element_type=jnp.float32,
        )
    logits = out[:16]
    value = out[16:17]
    side = side_ref[...]
    rewards, mu_logp, actions, next_start, learner = [side[i : i + 1] for i in range(5)]
    named = lax.broadcasted_iota(jnp.int32, (BLOCK, lanes), 0).astype(jnp.float32) == learner
    count = jnp.dot(
        counts_ref[...].astype(jnp.bfloat16),
        named.astype(jnp.bfloat16),
        preferred_element_type=jnp.float32,
    )[:1]
    weight = 1.0 / (jnp.maximum(count, 1.0) * STEPS)
    top = jnp.max(logits, axis=0, keepdims=True)
    shifted = jnp.exp(logits - top)
    total = jnp.sum(shifted, axis=0, keepdims=True)
    probs = shifted / total
    log_total = jnp.log(total) + top
    which = lax.broadcasted_iota(jnp.int32, logits.shape, 0).astype(jnp.float32)
    picked = (which == actions).astype(jnp.float32)
    logp = jnp.sum(picked * logits, axis=0, keepdims=True) - log_total
    rho = jnp.minimum(1.0, jnp.exp(logp - mu_logp))
    discount = GAMMA_RATE * (1.0 - next_start)
    lane = lax.broadcasted_iota(jnp.int32, value.shape, 1)
    last = lane >= lanes - agents

    def ahead(x, by):
        return pltpu.roll(x, lanes - by, 1)

    value_next = jnp.where(last, value, ahead(value, agents))
    acc = rho * (rewards + discount * value_next - value)
    factor = discount * rho
    by = agents
    while by < lanes:
        out_of = lane >= lanes - by
        acc = acc + factor * jnp.where(out_of, 0.0, ahead(acc, by))
        factor = factor * jnp.where(out_of, 0.0, ahead(factor, by))
        by *= 2
    targets = value + acc
    target_next = jnp.where(last, value, ahead(targets, agents))
    advantage = rho * (rewards + discount * target_next - value)
    d_logits = -(weight * advantage) * (picked - probs)
    d_value = weight * (value - targets)
    row = lax.broadcasted_iota(jnp.int32, (8, lanes), 0)
    d_tail = jnp.where(row == 0, d_value, 0.0)
    cot = jnp.concatenate([d_logits, d_tail], axis=0).astype(jnp.bfloat16)
    zeros = jnp.zeros((GRAD_ROWS, BLOCK), jnp.float32)
    for side_of in range(2):
        keep_ref[side_of] = zeros
        send_ref[side_of] = zeros
    core = place_ref[0]
    quarter = half // 2
    for side_of in range(2):
        for j in range(quarter):
            rows = slice(j * NUM_HEADS, (j + 1) * NUM_HEADS)
            for ref, who in ((keep_ref, core), (send_ref, 1 - core)):
                part = traj[side_of * half + who * quarter + j]
                out = jnp.dot(cot, part, preferred_element_type=jnp.float32)
                ref[side_of, rows, :] = out[:NUM_HEADS]


def rollout(table, rows_own, rows_other, obs, starts, terms_own, rec_own, parts_a, parts_b):
    steps = starts.shape[1]
    agents = starts.shape[0] // 2
    half = rec_own.shape[1]
    cols, width, lanes = 2 * half, half * BLOCK, steps * agents
    vmem, smem = [pl.BlockSpec(memory_space=m) for m in (pltpu.VMEM, pltpu.SMEM)]
    parts = list(parts_a) + list(parts_b)
    return pl.pallas_call(
        rollout_kernel,
        in_specs=[smem] * 3 + [vmem] * (4 + len(parts)),
        out_specs=[vmem] * 6,
        out_shape=[
            jax.ShapeDtypeStruct((cols, lanes, BLOCK), jnp.bfloat16),
            jax.ShapeDtypeStruct((agents, width), jnp.bfloat16),
            jax.ShapeDtypeStruct((agents, width), jnp.float32),
            jax.ShapeDtypeStruct((2 * agents, width), jnp.bfloat16),
            jax.ShapeDtypeStruct((PAD, BLOCK), jnp.float32),
            jax.ShapeDtypeStruct((HEAD_ROWS, width), jnp.bfloat16),
        ],
        scratch_shapes=[
            pltpu.VMEM((4, half, lanes, BLOCK), jnp.float32),
            pltpu.VMEM((4 * half, ROWS_A, BLOCK), jnp.bfloat16),
            pltpu.VMEM((4 * half, ROWS_B, BLOCK), jnp.bfloat16),
            pltpu.VMEM((steps, agents, BLOCK), jnp.float32),
            pltpu.VMEM((cols, agents, BLOCK), jnp.bfloat16),
            pltpu.VMEM((cols, agents, BLOCK), jnp.bfloat16),
            pltpu.VMEM((cols, agents, BLOCK), jnp.float32),
        ],
        compiler_params=pltpu.CompilerParams(vmem_limit_bytes=VMEM_LIMIT),
    )(table, rows_own, rows_other, obs, starts, terms_own, rec_own, *parts)


def head_grads(place, traj, head_own, head_other, side, counts):
    vmem = pl.BlockSpec(memory_space=pltpu.VMEM)
    return pl.pallas_call(
        head_kernel,
        in_specs=[pl.BlockSpec(memory_space=pltpu.SMEM)] + [vmem] * 5,
        out_specs=[vmem] * 2,
        out_shape=[jax.ShapeDtypeStruct((2, GRAD_ROWS, BLOCK), jnp.float32)] * 2,
        compiler_params=pltpu.CompilerParams(vmem_limit_bytes=SMALL_LIMIT),
    )(place, traj, head_own, head_other, side, counts)


def assemble_kernel(place_ref, grad_ref, mate_ref, out_ref):
    first = place_ref[0] == 0
    grad, mate = grad_ref[...], mate_ref[...]
    quarters = [jnp.where(first, grad, mate), jnp.where(first, mate, grad)]
    per = out_ref.shape[1] // (2 * BLOCK)
    for i in range(2):
        for j in range(per):
            c = i * per + j
            rows = slice(j * NUM_HEADS, (j + 1) * NUM_HEADS)
            out_ref[:, c * BLOCK : (c + 1) * BLOCK] = quarters[i][rows, :]


def assemble(place, grad, mate):
    vmem = pl.BlockSpec(memory_space=pltpu.VMEM)
    per = grad.shape[0] // NUM_HEADS
    return pl.pallas_call(
        assemble_kernel,
        in_specs=[pl.BlockSpec(memory_space=pltpu.SMEM)] + [vmem] * 2,
        out_specs=vmem,
        out_shape=jax.ShapeDtypeStruct((NUM_HEADS, 2 * per * BLOCK), jnp.float32),
    )(place, grad, mate)


def join_kernel(*refs):
    at = 0
    for ref in refs[:-1]:
        rows = ref.shape[0]
        refs[-1][at : at + rows, :] = ref[...]
        at += rows


def join(parts):
    vmem = pl.BlockSpec(memory_space=pltpu.VMEM)
    rows = sum([p.shape[0] for p in parts])
    return pl.pallas_call(
        join_kernel,
        in_specs=[vmem] * len(parts),
        out_specs=vmem,
        out_shape=jax.ShapeDtypeStruct((rows, BLOCK), parts[0].dtype),
    )(*parts)


def pack_kernel(where_ref, in_ref, head_ref, rec_ref, out_ref):
    obs_width = in_ref.shape[0]
    out_ref[obs_width + PAD :, :] = rec_ref[...]
    out_ref[:obs_width, :] = in_ref[...]
    at = pl.multiple_of(where_ref[0] * BLOCK, BLOCK)
    block = head_ref[:, pl.ds(at, BLOCK)].astype(jnp.float32)
    row = lax.broadcasted_iota(jnp.int32, (PAD, BLOCK), 0)
    low = jnp.where(row == 0, block[PAD : PAD + 1], 0.0)
    part = jnp.where(where_ref[1] == 0, block[:PAD], low)
    out_ref[obs_width : obs_width + PAD, :] = part.astype(jnp.bfloat16)


def pack(where, in_part, head, rec_part):
    vmem = pl.BlockSpec(memory_space=pltpu.VMEM)
    rows = in_part.shape[0] + PAD + rec_part.shape[0]
    return pl.pallas_call(
        pack_kernel,
        in_specs=[pl.BlockSpec(memory_space=pltpu.SMEM)] + [vmem] * 3,
        out_specs=vmem,
        out_shape=jax.ShapeDtypeStruct((rows, BLOCK), jnp.bfloat16),
    )(where, in_part, head, rec_part)


def swap(v, axis="blk"):
    return lax.ppermute(v, axis, [(0, 1), (1, 0)])


def ring(v, axis):
    size = lax.axis_size(axis)
    return [v] + [
        lax.ppermute(v, axis, [(i, (i + k) % size) for i in range(size)])
        for k in range(1, size)
    ]


def sum_over(v, axes):
    for axis in axes:
        v = sum(ring(v, axis)[1:], v)
    return v


def shards(
    observations,
    in_weight,
    rec_blocks,
    block_rows,
    episode_start,
    actions,
    rewards,
    mu_logp,
    head_weight,
    learner_of,
):
    blk = lax.axis_index("blk")
    num_agents, num_steps, obs_width = observations.shape
    mine = num_agents // 2
    cols = rec_blocks.shape[1]
    place_y, place_x, place_core = [lax.axis_index(a) for a in ("y", "x", "core")]
    gate, col = place_y, 2 * place_x + place_core
    in_part = lax.dynamic_slice(in_weight, (0, gate, col * BLOCK), (obs_width, 1, BLOCK))
    head_own = jnp.pad(head_weight.T, ((0, HEAD_ROWS - head_weight.shape[1]), (0, 0)))
    piece = (cols * gate + col) % (2 * cols)
    where = jnp.stack([piece // 2, piece % 2]).astype(jnp.int32)
    rec_part = lax.dynamic_slice(
        rec_blocks, (gate, col, 0, 0, 0), (1, 1) + rec_blocks.shape[2:]
    )
    packed = pack(
        where, in_part.reshape(-1, BLOCK), head_weight.T, rec_part.reshape(-1, BLOCK)
    )
    rows_own = block_rows.reshape(-1)
    packed, rows_other, learner = lax.optimization_barrier(
        (swap(packed), swap(rows_own), learner_of)
    )
    onehot = learner == jnp.arange(BLOCK, dtype=jnp.int32)[None, :]
    counts = jnp.sum(onehot.astype(jnp.bfloat16), axis=0, keepdims=True)
    counts = sum_over(jnp.broadcast_to(counts, (PAD, BLOCK)), ("z",))
    over_x = jnp.concatenate(ring(packed[:ROWS_A], "x"), axis=0)
    over_y = join(ring(packed[ROWS_A:], "y") + [counts])

    back = jnp.arange(4, dtype=jnp.int32)
    from_y, from_x = (place_y - back) % 4, (place_x - back) % 4
    from_core = jnp.stack([place_core, 1 - place_core])
    index = (
        8 * from_y[None, :, None] + 2 * from_x[None, None, :] + from_core[:, None, None]
    )
    table = jnp.concatenate(
        [
            index.reshape(-1),
            jnp.swapaxes(index, 1, 2).reshape(-1),
            jnp.stack([cols * blk, mine * blk]),
        ]
    ).astype(jnp.int32)

    starts = episode_start.astype(jnp.float32)
    next_start = jnp.concatenate([starts[:, 1:], jnp.zeros_like(starts[:, :1])], axis=1)
    side = jnp.stack(
        [
            rewards,
            mu_logp,
            actions.astype(jnp.float32),
            next_start,
            jnp.broadcast_to(learner_of.astype(jnp.float32), rewards.shape),
        ]
        + [jnp.zeros_like(rewards)] * 3
    )
    side = lax.dynamic_slice_in_dim(side, blk * mine, mine, 1)
    side = jnp.swapaxes(side, 1, 2).reshape(8, num_steps * mine)
    obs = lax.dynamic_slice_in_dim(observations, blk * mine, mine, 0)
    obs = jnp.swapaxes(obs, 0, 1).reshape(num_steps * mine, obs_width)

    over_x, over_y, obs, side, table, rows_own, rows_other = lax.optimization_barrier(
        (over_x, over_y, obs, side, table, rows_own, rows_other)
    )
    parts_a, parts_b, terms_own = lax.optimization_barrier(
        (ring(over_x, "y"), ring(over_y, "x"), input_terms(obs, in_weight))
    )
    parts_a = parts_a + [swap(p, "core") for p in parts_a]
    parts_b = parts_b + [swap(p, "core") for p in parts_b]

    traj, hidden_own, cell_own, states, counts, head_other = rollout(
        table, rows_own, rows_other, obs, episode_start, terms_own, rec_blocks, parts_a, parts_b
    )
    mate = place_core.reshape(1).astype(jnp.int32)
    kept, sent = head_grads(mate, traj, head_own, head_other, side, counts)
    kept = kept + swap(sent, "core")
    states = swap(states)
    grad = sum_over(kept[0] + swap(kept[1]), ("y", "x", "z"))
    grad_mate = swap(grad, "core")
    head_grad = assemble(mate, grad, grad_mate).T

    def place(here, there):
        first = jnp.where(blk == 0, here, there)
        second = jnp.where(blk == 0, there, here)
        return jnp.concatenate([first, second], axis=0)

    cell_last = place(cell_own, states[:mine].astype(jnp.float32))
    hidden_last = place(hidden_own, states[mine:])
    return (head_grad, hidden_last, cell_last)


def solution(mesh):
    fine = Mesh(mesh.devices.reshape(4, 4, 4, 2, 2), ("y", "x", "z", "core", "blk"))
    rows = TORUS
    return jax.shard_map(
        shards,
        mesh=fine,
        in_specs=(
            P(rows, None, None),
            P(None, None, "blk"),
            P(None, "blk", None, None, None),
            P(None, "blk", None),
            P(rows, None),
            P(rows, None),
            P(rows, None),
            P(rows, None),
            P("blk", None),
            P(rows, None),
        ),
        out_specs=(P("blk", None), P(rows, "blk"), P(rows, "blk")),
        check_vma=False,
    )
```
